512 devices in a mesh: replica: 16 (over z), outer: 32 (over x, y, core).
Axes of the slice: x: 4, y: 4, z: 16, core: 2. Of those that a mesh axis runs over, the one named last changes fastest.
Arguments:
- activations: bfloat16 [65536, 4096], P(('replica', 'outer')), may hold values from -6 to 6
- grad_hidden: bfloat16 [65536, 112], P(('replica', 'outer')), may hold values from -0.125 to 0.125
- labels: int32 [65536], P(('replica', 'outer')), may hold values from -100 to 128255, as said below
- lengths: int32 [512, 8], P(('replica', 'outer')), may hold values from 1 to 64, 128 in all within a row
- error_state: float32 [512, 2, 56, 4096], P(('replica', 'outer')), may hold values from -1.5 to 1.5
- warm_start: float32 [2, 8, 4096], replicated, may hold values from -6 to 6
Outputs:
- left_factor: float32 [2, 56, 8], replicated
- right_factor: float32 [2, 8, 4096], replicated
- new_error: float32 [512, 2, 56, 4096], P(('replica', 'outer'))
The draws below stay inside these ranges and needn't reach their ends.
Inputs may be any that keep to these rules, and one draw needn't show every extreme that they name: `labels`: -100 marks a token without a target; other values are token ids. Every token of the first worker has a target.
All inputs are finite; a program needn't handle non-finite values.
Results may differ from the reference program's by a relative error of at most 0.0095.
Values sent between devices are 32-bit elements; how exact they have to be, the bound alone decides.
No kernel may reach another device: no remote copies, remote signals or barrier semaphores. Data moves between devices by JAX's collectives and lax.ppermute only.
A program may use at most 64 MiB of HBM per device.

```python
import math
import jax
import jax.numpy as jnp
import numpy as np
from jax import lax

DW = 4096
HID = 56
RANK = 8
VOCAB = 128256
DOCS = 8
TOK_DEV = 128
WORKERS = 512
TOKENS = 65536


def draw_labels(key, part):
    key = jax.random.fold_in(key, 11)
    first_key, second_key, level_key, gate_key, worker_key = jax.random.split(key, 5)
    places = jnp.arange(TOKENS, dtype=jnp.int32)
    tickets = jax.random.randint(first_key, (TOKENS,), 0, TOKENS, dtype=jnp.int32)
    token_ids = jax.random.randint(second_key, (TOKENS,), 0, VOCAB, dtype=jnp.int32)
    level = jax.random.randint(level_key, (), 200, 951, dtype=jnp.int32)
    gate_tickets = jax.random.randint(gate_key, (TOKENS,), 0, 1000, dtype=jnp.int32)
    worker_tickets = jax.random.randint(worker_key, (WORKERS,), 0, 8, dtype=jnp.int32)
    owners = (places // TOK_DEV).astype(jnp.int32)
    dropped = worker_tickets[owners] == 0
    base_keep = jnp.logical_or(places % 4 == 0, tickets >= places)
    gated = jnp.logical_and(base_keep, gate_tickets < level)
    gated = jnp.logical_and(gated, jnp.logical_not(dropped))
    keeping = jnp.logical_or(places < TOK_DEV, gated)
    result = jnp.where(keeping, token_ids, -100)
    result = jnp.where(places == TOKENS - 1, VOCAB - 1, result)
    result = jnp.where(places == TOKENS - 2, -100, result)
    return result.astype(jnp.int32)


def level_of(key, dims, cuts, least, top_value):
    def one(dim, blocks):
        draws = jax.random.uniform(jax.random.fold_in(jax.random.fold_in(key, 6), dim), (blocks,), jnp.float32, least / len(cuts), top_value / len(cuts))
        return jnp.repeat(jnp.exp(draws), dims[dim] // blocks).reshape((-1,) + (1,) * (len(dims) - dim - 1))

    level = one(*cuts[0])
    for cut in cuts[1:]:
        level = level * one(*cut)
    return level


def length_profile(amount, total, reach, skew):
    weights = [(1 << 20) // math.isqrt(standing ** skew) + 1 for standing in range(2, amount + 1)]
    surplus, counts = total - reach - (amount - 1), [1] * (amount - 1)
    while surplus > 0:
        movable = [i for i in range(amount - 1) if counts[i] < reach]
        mass, left = sum([weights[i] for i in movable]), surplus
        for i in movable:
            addition = min(reach - counts[i], max(1, left * weights[i] // mass), surplus)
            counts[i] = counts[i] + addition
            surplus = surplus - addition
    return np.array([reach] + counts)


def ragged(stream_key, number_of, total, most, lean):
    if number_of == 2:
        one = jax.random.randint(stream_key, (), max(1, total - most), min(most, total - 1) + 1)
        return jnp.stack([one, total - one])
    sizes = jnp.asarray(length_profile(number_of, total, most, lean), jnp.int32)
    pairs = (number_of - 1) // 2
    source_of, taker = sizes[1:1 + 2 * pairs:2], sizes[2:2 + 2 * pairs:2]
    slack = jnp.minimum(source_of - 1, most - taker)
    passed = jax.random.randint(jax.random.fold_in(stream_key, 1), (pairs,), 0, 1 << 20) % (slack + 1)
    sizes = sizes.at[1:1 + 2 * pairs:2].set(source_of - passed).at[2:2 + 2 * pairs:2].set(taker + passed)
    return sizes[jax.random.permutation(jax.random.fold_in(stream_key, 2), number_of)]


def scatter_about(stream_key, extent, spread, limit, cuts=(), kind=jnp.bfloat16):
    values = spread * jax.random.normal(stream_key, extent, jnp.float32)
    if cuts:
        values = values * level_of(stream_key, extent, cuts, -0.22, 0.18)
    return jnp.clip(values, -limit, limit).astype(kind)


def setup_inputs(seed: int = 0) -> dict:
    seeds = jax.random.split(jax.random.key(seed), 7)
    return {
        "activations": scatter_about(seeds[0], (TOKENS, DW), 1.0, 6.0, ((0, 512),)),
        "grad_hidden": scatter_about(seeds[1], (TOKENS, 2 * HID), (0.1 / TOK_DEV ** 0.5), 0.125, ((0, 512),)),
        "labels": draw_labels(jax.random.fold_in(seeds[6], 71), 0),
        "lengths": jax.vmap(lambda own: ragged(own, DOCS, TOK_DEV, TOK_DEV // 2, 2))(jax.random.split(seeds[3], WORKERS)).reshape((WORKERS, DOCS)).astype(jnp.int32),
        "error_state": scatter_about(seeds[4], (WORKERS, 2, HID, DW), 0.1, 1.5, ((0, 512),), jnp.float32),
        "warm_start": scatter_about(seeds[5], (2, RANK, DW), 1.0, 6.0, (), jnp.float32),
    }


def token_mask(labels_row, lengths_row):
    places = jnp.arange(labels_row.shape[0], dtype=jnp.int32)
    finals = (jnp.cumsum(lengths_row) - 1).astype(jnp.int32)
    at_final = jnp.any(places[:, None] == finals[None, :], axis=1)
    return jnp.logical_and(labels_row != -100, jnp.logical_not(at_final))

def worker_raw(acts_rows, grad_rows, valid_mask):
    masked = jnp.where(valid_mask[:, None], grad_rows, jnp.zeros_like(grad_rows))
    raw_sum = lax.dot_general(masked, acts_rows, (((0,), (0,)), ((), ())), preferred_element_type=jnp.float32)
    raw_sum = raw_sum.astype(jnp.bfloat16)
    return raw_sum.astype(jnp.float32).reshape(2, HID, DW)

def orthonormal(p_sum):
    basis = []
    for column in range(p_sum.shape[2]):
        vector = p_sum[:, :, column]
        for earlier in basis:
            vector = vector - lax.optimization_barrier(jnp.sum(earlier * vector, axis=1, keepdims=True)) * earlier
        vector = vector / (jnp.sqrt(lax.optimization_barrier(jnp.sum(vector * vector, axis=1, keepdims=True))) + 1e-08)
        basis.append(vector)
    return jnp.stack(basis, axis=2)

def reference(activations, grad_hidden, labels, lengths, error_state, warm_start):
    acts_all = activations.reshape(WORKERS, TOK_DEV, DW)
    grad_all = grad_hidden.reshape(WORKERS, TOK_DEV, 2 * HID)
    labels_all = labels.reshape(WORKERS, TOK_DEV)
    valid_all = jax.vmap(token_mask)(labels_all, lengths)
    total_valid = jnp.sum(valid_all.astype(jnp.float32))
    factor = jnp.float32(TOKENS) / total_valid
    highest = lax.Precision.HIGHEST

    def merged_of(pieces):
        acts_rows, grad_rows, valid_mask, carried = pieces
        return factor * worker_raw(acts_rows, grad_rows, valid_mask) + carried
    pieces = (acts_all, grad_all, valid_all, error_state)

    def p_step(carry, piece):
        merged = merged_of(piece)
        return (carry + jnp.einsum('ghc,grc->ghr', merged, warm_start, precision=highest), None)
    p_sum, _ = lax.scan(p_step, jnp.zeros((2, HID, RANK), jnp.float32), pieces)
    left_factor = orthonormal(p_sum)

    def q_step(carry, piece):
        merged = merged_of(piece)
        return (carry + jnp.einsum('ghc,ghr->grc', merged, left_factor, precision=highest), None)
    right_factor, _ = lax.scan(q_step, jnp.zeros((2, RANK, DW), jnp.float32), pieces)
    approx = jnp.einsum('ghr,grc->ghc', left_factor, right_factor, precision=highest)

    def error_step(piece):
        return merged_of(piece) - approx / WORKERS
    new_error = lax.map(error_step, pieces)
    return (left_factor, right_factor, new_error)
```

```python
import jax
import jax.numpy as jnp
from jax import lax
from jax.sharding import PartitionSpec as P

BOTH = ("replica", "outer")


def token_mask(labels, lengths_row):
    places = jnp.arange(labels.shape[0], dtype=jnp.int32)
    finals = jnp.cumsum(lengths_row) - 1
    at_final = jnp.any(places[:, None] == finals[None, :], axis=1)
    return jnp.logical_and(labels != -100, jnp.logical_not(at_final))


def orthonormal(p_sum):
    basis = []
    for column in range(p_sum.shape[2]):
        vector = p_sum[:, :, column]
        for earlier in basis:
            vector = vector - jnp.sum(earlier * vector, axis=1, keepdims=True) * earlier
        vector = vector / (jnp.sqrt(jnp.sum(vector * vector, axis=1, keepdims=True)) + 1e-08)
        basis.append(vector)
    return jnp.stack(basis, axis=2)


def project(matrix, warm_start):
    return jnp.einsum("ghc,grc->ghr", matrix, warm_start, precision=lax.Precision.HIGHEST)


def exchange(blocks, axis):
    return lax.all_to_all(blocks, axis, 0, 0, tiled=True)


def everyone(block, axis):
    return exchange(jnp.broadcast_to(block[None], (lax.axis_size(axis),) + block.shape), axis)


def local(activations, grad_hidden, labels, lengths, error_state, warm_start):
    matrices, rank, features = warm_start.shape
    hidden = error_state.shape[2]
    valid_mask = token_mask(labels, lengths[0])
    local_count = jnp.sum(valid_mask.astype(jnp.float32))
    masked = jnp.where(valid_mask[:, None], grad_hidden, jnp.zeros_like(grad_hidden))
    raw_sum = lax.dot_general(
        masked, activations, (((0,), (0,)), ((), ())), preferred_element_type=jnp.float32
    )
    raw_sum = raw_sum.astype(jnp.bfloat16)
    raw_full = raw_sum.astype(jnp.float32).reshape(matrices, hidden, features)
    carried = error_state[0]
    workers = lax.axis_size("replica") * lax.axis_size("outer")
    all_tokens = float(activations.shape[0] * workers)
    terms = jnp.stack([project(raw_full, warm_start), project(carried, warm_start)]).reshape(-1, 128)
    count_row = jnp.full((1, 128), local_count, jnp.float32)
    payload = jnp.concatenate([terms, count_row, jnp.zeros((1, 128), jnp.float32)], axis=0)
    for axis in ("outer", "replica"):
        payload = jnp.sum(everyone(payload, axis), axis=0)
    total_valid = payload[terms.shape[0], 0]
    factor = all_tokens / total_valid
    sums = payload[: terms.shape[0]].reshape(2, matrices, hidden, rank)
    left_factor = orthonormal(factor * sums[0] + sums[1])
    merged = factor * raw_full + carried
    q_local = jnp.einsum("ghc,ghr->grc", merged, left_factor, precision=lax.Precision.HIGHEST)
    outer = lax.axis_size("outer")
    blocks = q_local.reshape(matrices * rank, outer, features // outer).transpose(1, 0, 2)
    block = jnp.sum(exchange(blocks, "outer"), axis=0)
    block = jnp.sum(everyone(block, "replica"), axis=0)
    right_factor = everyone(block, "outer").transpose(1, 0, 2).reshape(matrices, rank, features)
    approx = jnp.einsum("ghr,grc->ghc", left_factor, right_factor, precision=lax.Precision.HIGHEST)
    new_error = merged - approx / workers
    return (left_factor, right_factor, new_error[None])


def solution(mesh):
    placed = (
        P(BOTH, None),
        P(BOTH, None),
        P(BOTH),
        P(BOTH, None),
        P(BOTH, None, None, None),
        P(),
    )
    return jax.shard_map(
        local,
        mesh=mesh,
        in_specs=placed,
        out_specs=(P(), P(), P(BOTH, None, None, None)),
        check_vma=False,
    )
```

```python
import functools

import jax
import jax.numpy as jnp
from jax import lax
from jax.experimental import pallas as pl
from jax.experimental.pallas import tpu as pltpu
from jax.sharding import PartitionSpec as P

BOTH = ("replica", "outer")
F32, BF16 = jnp.float32, jnp.bfloat16
HALF = 64
TILE = 1024


def halves(x):
    high = x.astype(BF16)
    return high, (x - high.astype(F32)).astype(BF16)


def padded(first, second):
    gap = jnp.zeros((HALF - first.shape[0], first.shape[1]), first.dtype)
    return jnp.concatenate([first, gap, second, gap], axis=0)


def dot(a, b):
    return lax.dot_general(a, b, (((1,), (0,)), ((), ())), preferred_element_type=F32)


def dot_rows(a, b):
    return lax.dot_general(a, b, (((1,), (1,)), ((), ())), preferred_element_type=F32)


def terms_kernel(len_ref, label_ref, grad_ref, act_ref, err_ref, warm_ref, raw_ref, pay_ref, masked_ref):
    hidden = err_ref.shape[2]
    rank = warm_ref.shape[1]
    lane = lax.broadcasted_iota(jnp.int32, (1, 128), 1)

    @pl.when(pl.program_id(0) == 0)
    def _():
        mask = label_ref[...] != -100
        final = -1
        for document in range(len_ref.shape[1]):
            final = final + len_ref[0, document]
            mask = jnp.logical_and(mask, lane != final)
        grad = grad_ref[...].astype(F32)
        grad = padded(grad[:hidden], grad[hidden:])
        masked_ref[...] = jnp.where(mask, grad, 0.0).astype(BF16)
        count = jnp.sum(mask.astype(F32), axis=1, keepdims=True)
        row = lax.broadcasted_iota(jnp.int32, pay_ref.shape, 0)
        at = jnp.logical_and(row == 0, lane == 127)
        pay_ref[...] = jnp.where(at, count, 0.0)

    raw = dot(masked_ref[...], act_ref[...]).astype(BF16)
    raw_ref[...] = raw
    warm = warm_ref[...].reshape(2 * rank, warm_ref.shape[2])
    high = warm.astype(BF16)
    rest = warm - high.astype(F32)
    middle, low = halves(rest)
    split = jnp.concatenate([high, middle, low], axis=0)
    of_raw = dot_rows(split, raw)
    n = 2 * rank
    of_raw = of_raw[:n] + (of_raw[n : 2 * n] + of_raw[2 * n :])
    carried_high, carried_low = halves(padded(err_ref[0, 0], err_ref[0, 1]))
    of_err = dot_rows(split[: 2 * n], carried_high)
    of_err = of_err[:n] + (of_err[n:] + dot_rows(high, carried_low))
    left = lane < HALF
    pay_ref[:rank] += jnp.where(left, of_raw[:rank], of_raw[rank:])
    pay_ref[rank:] += jnp.where(left, of_err[:rank], of_err[rank:])


def basis_of(vectors):
    row = lax.broadcasted_iota(jnp.int32, (vectors.shape[0], 1), 0)
    for r in range(vectors.shape[0]):
        current = vectors[r : r + 1]
        dots = jnp.sum(vectors * current, axis=1, keepdims=True)
        norm = jnp.sqrt(dots[r : r + 1]) + 1e-08
        unit = current / norm
        later = vectors - (dots / norm) * unit
        vectors = jnp.where(row == r, unit, jnp.where(row > r, later, vectors))
    return vectors


def factor_of(pay_ref, all_tokens):
    return all_tokens / pay_ref[0:1, 127:128]


def right_kernel(all_tokens, pay_ref, raw_ref, err_ref, left_ref, basis_ref, q_ref, lhs_ref):
    rank = pay_ref.shape[0] // 2
    hidden = err_ref.shape[2]
    factor = factor_of(pay_ref, all_tokens)

    @pl.when(pl.program_id(0) == 0)
    def _():
        lane = lax.broadcasted_iota(jnp.int32, (1, 128), 1)
        p_sum = factor * pay_ref[:rank] + pay_ref[rank:]
        first = basis_of(jnp.where(lane < hidden, p_sum, 0.0))
        of_second = jnp.logical_and(lane >= HALF, lane < HALF + hidden)
        second = basis_of(jnp.where(of_second, p_sum, 0.0))
        left_ref[0] = first[:, :hidden]
        left_ref[1] = pltpu.roll(second, HALF, 1)[:, :hidden]
        basis = jnp.concatenate([first, second], axis=0)
        basis_ref[...] = basis
        high, low = halves(basis)
        top = jnp.concatenate([high, high], axis=1)
        bottom = jnp.concatenate([low, jnp.zeros_like(low)], axis=1)
        lhs_ref[...] = jnp.concatenate([top, bottom], axis=0)

    merged = factor * raw_ref[...].astype(F32) + padded(err_ref[0, 0], err_ref[0, 1])
    high, low = halves(merged)
    both = dot(lhs_ref[...], jnp.concatenate([high, low], axis=0))
    q_local = both[: 2 * rank] + both[2 * rank :]
    width = q_ref.shape[2]
    for block in range(q_ref.shape[0]):
        q_ref[block] = q_local[:, block * width : (block + 1) * width]


def error_kernel(all_tokens, workers, pay_ref, basis_ref, sum_ref, raw_ref, err_ref, right_ref, new_ref, lhs_ref):
    rank = pay_ref.shape[0] // 2
    hidden = err_ref.shape[2]

    @pl.when(pl.program_id(0) == 0)
    def _():
        high, low = halves(basis_ref[...])
        high, low = high.astype(F32), low.astype(F32)
        gap = jnp.zeros((128 - 6 * rank, 128), F32)
        stacked = jnp.concatenate([high, high, low, gap], axis=0)
        lhs_ref[...] = stacked.T.astype(BF16)

    summed = jnp.concatenate([sum_ref[block] for block in range(sum_ref.shape[0])], axis=1)
    right_ref[0] = summed[:rank]
    right_ref[1] = summed[rank:]
    high, low = halves(summed * (1.0 / workers))
    gap = jnp.zeros((128 - 6 * rank, high.shape[1]), BF16)
    approx = dot(lhs_ref[...], jnp.concatenate([high, low, high, gap], axis=0))
    factor = factor_of(pay_ref, all_tokens)
    for matrix in range(2):
        rows = slice(matrix * HALF, matrix * HALF + HALF)
        raw = raw_ref[rows, :].astype(F32)[:hidden]
        new_ref[0, matrix] = factor * raw + err_ref[0, matrix] - approx[rows][:hidden]


def exchange(blocks, axis):
    return lax.all_to_all(blocks, axis, 0, 0, tiled=True)


def everyone(block, axis):
    return exchange(jnp.broadcast_to(block[None], (lax.axis_size(axis),) + block.shape), axis)


def whole(shape):
    return pl.BlockSpec(shape, lambda i: (0,) * len(shape))


def local(activations, grad_hidden, labels, lengths, error_state, warm_start):
    matrices, rank, features = warm_start.shape
    hidden = error_state.shape[2]
    tokens = activations.shape[0]
    outer = lax.axis_size("outer")
    workers = lax.axis_size("replica") * outer
    all_tokens = float(tokens * workers)
    width = features // outer
    grid = (features // TILE,)
    params = pltpu.CompilerParams(vmem_limit_bytes=24 * 2**20)
    err_spec = pl.BlockSpec((1, matrices, hidden, TILE), lambda i: (0, 0, 0, i))
    raw_spec = pl.BlockSpec((2 * HALF, TILE), lambda i: (0, i))
    warm_spec = pl.BlockSpec((matrices, rank, TILE), lambda i: (0, 0, i))
    block_spec = pl.BlockSpec((TILE // width, 2 * rank, width), lambda i: (i, 0, 0))
    raw, payload = pl.pallas_call(
        terms_kernel,
        grid=grid,
        in_specs=[
            pl.BlockSpec(memory_space=pltpu.SMEM),
            whole((1, tokens)),
            whole((matrices * hidden, tokens)),
            pl.BlockSpec((tokens, TILE), lambda i: (0, i)),
            err_spec,
            warm_spec,
        ],
        out_specs=[raw_spec, whole((2 * rank, 128))],
        out_shape=[
            jax.ShapeDtypeStruct((2 * HALF, features), BF16),
            jax.ShapeDtypeStruct((2 * rank, 128), F32),
        ],
        scratch_shapes=[pltpu.VMEM((2 * HALF, tokens), BF16)],
        compiler_params=params,
        name="terms",
    )(lengths, labels.reshape(1, tokens), grad_hidden.T, activations, error_state, warm_start)
    for axis in ("outer", "replica"):
        payload = jnp.sum(everyone(payload, axis), axis=0)
    left_rows, basis, q_local = pl.pallas_call(
        functools.partial(right_kernel, all_tokens),
        grid=grid,
        in_specs=[whole((2 * rank, 128)), raw_spec, err_spec],
        out_specs=[whole((matrices, rank, hidden)), whole((2 * rank, 128)), block_spec],
        out_shape=[
            jax.ShapeDtypeStruct((matrices, rank, hidden), F32),
            jax.ShapeDtypeStruct((2 * rank, 128), F32),
            jax.ShapeDtypeStruct((outer, 2 * rank, width), F32),
        ],
        scratch_shapes=[pltpu.VMEM((4 * rank, 256), BF16)],
        compiler_params=params,
        name="right",
    )(payload, raw, error_state)
    block = jnp.sum(exchange(q_local, "outer"), axis=0)
    block = jnp.sum(everyone(block, "replica"), axis=0)
    summed = everyone(block, "outer")
    right_factor, new_error = pl.pallas_call(
        functools.partial(error_kernel, all_tokens, workers),
        grid=grid,
        in_specs=[whole((2 * rank, 128)), whole((2 * rank, 128)), block_spec, raw_spec, err_spec],
        out_specs=[warm_spec, err_spec],
        out_shape=[
            jax.ShapeDtypeStruct((matrices, rank, features), F32),
            jax.ShapeDtypeStruct((1, matrices, hidden, features), F32),
        ],
        scratch_shapes=[pltpu.VMEM((2 * HALF, 128), BF16)],
        compiler_params=params,
        name="error",
    )(payload, basis, summed, raw, error_state)
    return (left_rows.transpose(0, 2, 1), right_factor, new_error)


def solution(mesh):
    placed = (
        P(BOTH, None),
        P(BOTH, None),
        P(BOTH),
        P(BOTH, None),
        P(BOTH, None, None, None),
        P(),
    )
    return jax.shard_map(
        local,
        mesh=mesh,
        in_specs=placed,
        out_specs=(P(), P(), P(BOTH, None, None, None)),
        check_vma=False,
    )
```

```python
import functools

import jax
import jax.numpy as jnp
from jax import lax
from jax.experimental import pallas as pl
from jax.experimental.pallas import tpu as pltpu
from jax.sharding import PartitionSpec as P

BOTH = ("replica", "outer")
F32, BF16 = jnp.float32, jnp.bfloat16
HALF = 64
TILE = 1024


def halves(x):
    high = x.astype(BF16)
    return high, (x - high.astype(F32)).astype(BF16)


def padded(first, second):
    gap = jnp.zeros((HALF - first.shape[0], first.shape[1]), first.dtype)
    return jnp.concatenate([first, gap, second, gap], axis=0)


def dot(a, b):
    return lax.dot_general(a, b, (((1,), (0,)), ((), ())), preferred_element_type=F32)


def dot_rows(a, b):
    return lax.dot_general(a, b, (((1,), (1,)), ((), ())), preferred_element_type=F32)


def terms_kernel(len_ref, label_ref, grad_ref, act_ref, err_ref, warm_ref, raw_ref, pay_ref):
    hidden = err_ref.shape[2]
    rank = warm_ref.shape[1]
    n = 2 * rank
    lane = lax.broadcasted_iota(jnp.int32, (1, 128), 1)
    mask = label_ref[...] != -100
    final = -1
    for document in range(len_ref.shape[1]):
        final = final + len_ref[0, document]
        mask = jnp.logical_and(mask, lane != final)
    count = jnp.sum(mask.astype(F32), axis=1, keepdims=True)
    grad = grad_ref[...].astype(F32)
    grad = padded(grad[:hidden], grad[hidden:])
    masked = jnp.where(mask, grad, 0.0).astype(BF16)
    raw = dot(masked, act_ref[...]).astype(BF16)
    raw_ref[...] = raw
    warm = warm_ref[...].reshape(n, warm_ref.shape[2])
    high = warm.astype(BF16)
    middle, low = halves(warm - high.astype(F32))
    split = jnp.concatenate([high, middle, low], axis=0)
    of_raw = dot_rows(split, raw)
    of_raw = of_raw[:n] + (of_raw[n : 2 * n] + of_raw[2 * n :])
    carried_high, carried_low = halves(padded(err_ref[0, 0], err_ref[0, 1]))
    of_err = dot_rows(split[: 2 * n], carried_high)
    of_err = of_err[:n] + (of_err[n:] + dot_rows(high, carried_low))
    left = lane < HALF
    row = lax.broadcasted_iota(jnp.int32, (rank, 128), 0)
    at_count = jnp.logical_and(row == 0, lane == 127)
    pay_ref[:rank] = jnp.where(at_count, count, jnp.where(left, of_raw[:rank], of_raw[rank:]))
    pay_ref[rank:] = jnp.where(left, of_err[:rank], of_err[rank:])


def basis_of(vectors):
    row = lax.broadcasted_iota(jnp.int32, (vectors.shape[0], 1), 0)
    for r in range(vectors.shape[0]):
        current = vectors[r : r + 1]
        dots = jnp.sum(vectors * current, axis=1, keepdims=True)
        norm = jnp.sqrt(dots[r : r + 1]) + 1e-08
        unit = current / norm
        later = vectors - (dots / norm) * unit
        vectors = jnp.where(row == r, unit, jnp.where(row > r, later, vectors))
    return vectors


def factor_of(pay_ref, all_tokens):
    return all_tokens / pay_ref[0:1, 127:128]


def right_kernel(all_tokens, pay_ref, raw_ref, err_ref, left_ref, basis_ref, q_ref):
    rank = pay_ref.shape[0] // 2
    hidden = err_ref.shape[2]
    factor = factor_of(pay_ref, all_tokens)
    lane = lax.broadcasted_iota(jnp.int32, (1, 128), 1)
    p_sum = factor * pay_ref[:rank] + pay_ref[rank:]
    first = basis_of(jnp.where(lane < hidden, p_sum, 0.0))
    of_second = jnp.logical_and(lane >= HALF, lane < HALF + hidden)
    second = basis_of(jnp.where(of_second, p_sum, 0.0))
    left_ref[0] = first[:, :hidden]
    left_ref[1] = pltpu.roll(second, HALF, 1)[:, :hidden]
    basis = jnp.concatenate([first, second], axis=0)
    basis_ref[...] = basis
    high, low = halves(basis)
    top = jnp.concatenate([high, high], axis=1)
    bottom = jnp.concatenate([low, jnp.zeros_like(low)], axis=1)
    lhs = jnp.concatenate([top, bottom], axis=0)
    width = q_ref.shape[2]
    for part in range(raw_ref.shape[1] // TILE):
        at = pl.ds(part * TILE, TILE)
        carried = padded(err_ref[0, 0, :, at], err_ref[0, 1, :, at])
        high, low = halves(factor * raw_ref[:, at].astype(F32) + carried)
        both = dot(lhs, jnp.concatenate([high, low], axis=0))
        q_local = both[: 2 * rank] + both[2 * rank :]
        for block in range(TILE // width):
            q_ref[part * (TILE // width) + block] = q_local[:, block * width : (block + 1) * width]


def error_kernel(
    all_tokens, workers, pay_ref, basis_ref, sum_ref, raw_ref, err_ref, right_hbm, new_hbm,
    right_ref, new_ref, sems,
):
    rank = pay_ref.shape[0] // 2
    hidden = err_ref.shape[2]
    width = sum_ref.shape[2]
    high, low = halves(basis_ref[...])
    high, low = high.astype(F32), low.astype(F32)
    gap = jnp.zeros((128 - 6 * rank, 128), F32)
    lhs = jnp.concatenate([high, high, low, gap], axis=0).T.astype(BF16)
    factor = factor_of(pay_ref, all_tokens)
    copies = []
    for part in range(raw_ref.shape[1] // TILE):
        at = pl.ds(part * TILE, TILE)
        blocks = TILE // width
        summed = jnp.concatenate([sum_ref[part * blocks + block] for block in range(blocks)], axis=1)
        right_ref[0, :, at] = summed[:rank]
        right_ref[1, :, at] = summed[rank:]
        copies.append(pltpu.make_async_copy(right_ref.at[:, :, at], right_hbm.at[:, :, at], sems.at[0, part]))
        copies[-1].start()
        high, low = halves(summed * (1.0 / workers))
        gap = jnp.zeros((128 - 6 * rank, TILE), BF16)
        approx = dot(lhs, jnp.concatenate([high, low, high, gap], axis=0))
        for matrix in range(2):
            rows = slice(matrix * HALF, matrix * HALF + HALF)
            raw = raw_ref[rows, at].astype(F32)[:hidden]
            new_ref[0, matrix, :, at] = factor * raw + err_ref[0, matrix, :, at] - approx[rows][:hidden]
        copies.append(pltpu.make_async_copy(new_ref.at[:, :, :, at], new_hbm.at[:, :, :, at], sems.at[1, part]))
        copies[-1].start()
    for each in copies:
        each.wait()


def exchange(blocks, axis):
    return lax.all_to_all(blocks, axis, 0, 0, tiled=True)


def everyone(block, axis):
    return exchange(jnp.broadcast_to(block[None], (lax.axis_size(axis),) + block.shape), axis)


ANY = pl.BlockSpec(memory_space=pl.ANY)
VMEM = pl.BlockSpec(memory_space=pltpu.VMEM)
LIMIT = 16 * 2**20


def terms(lengths, labels, grad, activations, error_state, warm_start):
    _, rank, features = warm_start.shape
    operands = (labels, grad, activations, error_state, warm_start)
    raw = jax.ShapeDtypeStruct((2 * HALF, features), BF16)
    payload = jax.ShapeDtypeStruct((2 * rank, 128), F32)

    def once(x):
        return pl.BlockSpec(x.shape, lambda i: (0,) * len(x.shape))

    return pl.pallas_call(
        terms_kernel,
        grid=(1,),
        in_specs=[pl.BlockSpec(memory_space=pltpu.SMEM)] + [once(x) for x in operands],
        out_specs=[once(raw), once(payload)],
        out_shape=[raw, payload],
        name="terms",
    )(lengths, *operands)


def right(all_tokens, outer, payload, raw, error_state):
    rank = payload.shape[0] // 2
    hidden, features = error_state.shape[2:]
    return pl.pallas_call(
        functools.partial(right_kernel, all_tokens),
        in_specs=[VMEM] * 3,
        out_specs=[VMEM] * 3,
        out_shape=[
            jax.ShapeDtypeStruct((2, rank, hidden), F32),
            jax.ShapeDtypeStruct((2 * rank, 128), F32),
            jax.ShapeDtypeStruct((outer, 2 * rank, features // outer), F32),
        ],
        compiler_params=pltpu.CompilerParams(vmem_limit_bytes=LIMIT),
        name="right",
    )(payload, raw, error_state)


def error(all_tokens, workers, payload, basis, summed, raw, error_state):
    rank = payload.shape[0] // 2
    features = error_state.shape[3]
    right_factor = jax.ShapeDtypeStruct((2, rank, features), F32)
    return pl.pallas_call(
        functools.partial(error_kernel, all_tokens, workers),
        in_specs=[VMEM] * 5,
        out_specs=[ANY] * 2,
        out_shape=[right_factor, jax.ShapeDtypeStruct(error_state.shape, F32)],
        scratch_shapes=[
            pltpu.VMEM(right_factor.shape, F32),
            pltpu.VMEM(error_state.shape, F32),
            pltpu.SemaphoreType.DMA((2, features // TILE)),
        ],
        compiler_params=pltpu.CompilerParams(vmem_limit_bytes=LIMIT),
        name="error",
    )(payload, basis, summed, raw, error_state)


def local(activations, grad_hidden, labels, lengths, error_state, warm_start):
    outer = lax.axis_size("outer")
    workers = lax.axis_size("replica") * outer
    all_tokens = float(activations.shape[0] * workers)
    raw, payload = terms(
        lengths, labels.reshape(1, -1), grad_hidden.T, activations, error_state, warm_start
    )
    for axis in ("outer", "replica"):
        payload = jnp.sum(everyone(payload, axis), axis=0)
    left_rows, basis, q_local = right(all_tokens, outer, payload, raw, error_state)
    block = jnp.sum(exchange(q_local, "outer"), axis=0)
    block = jnp.sum(everyone(block, "replica"), axis=0)
    summed = everyone(block, "outer")
    right_factor, new_error = error(
        all_tokens, workers, payload, basis, summed, raw, error_state
    )
    return (left_rows.transpose(0, 2, 1), right_factor, new_error)


def solution(mesh):
    placed = (
        P(BOTH, None),
        P(BOTH, None),
        P(BOTH),
        P(BOTH, None),
        P(BOTH, None, None, None),
        P(),
    )
    return jax.shard_map(
        local,
        mesh=mesh,
        in_specs=placed,
        out_specs=(P(), P(), P(BOTH, None, None, None)),
        check_vma=False,
    )
```

```python
import functools

import jax
import jax.numpy as jnp
from jax import lax
from jax.experimental import pallas as pl
from jax.experimental.pallas import tpu as pltpu
from jax.sharding import Mesh, PartitionSpec as P

ALL = ("replica", "chip", "core")
OUTER = ("chip", "core")
F32, BF16 = jnp.float32, jnp.bfloat16
HALF = 64
TILE = 1024


def halves(x):
    high = x.astype(BF16)
    return high, (x - high.astype(F32)).astype(BF16)


def padded(first, second):
    gap = jnp.zeros((HALF - first.shape[0], first.shape[1]), first.dtype)
    return jnp.concatenate([first, gap, second, gap], axis=0)


def dot(a, b):
    return lax.dot_general(a, b, (((1,), (0,)), ((), ())), preferred_element_type=F32)


def dot_rows(a, b):
    return lax.dot_general(a, b, (((1,), (1,)), ((), ())), preferred_element_type=F32)


def terms_kernel(len_ref, label_ref, grad_ref, act_ref, err_ref, warm_ref, raw_ref, pay_ref):
    hidden = err_ref.shape[2]
    rank = warm_ref.shape[1]
    n = 2 * rank
    lane = lax.broadcasted_iota(jnp.int32, (1, 128), 1)
    mask = label_ref[...] != -100
    final = -1
    for document in range(len_ref.shape[1]):
        final = final + len_ref[0, document]
        mask = jnp.logical_and(mask, lane != final)
    count = jnp.sum(mask.astype(F32), axis=1, keepdims=True)
    grad = grad_ref[...].astype(F32)
    grad = padded(grad[:hidden], grad[hidden:])
    masked = jnp.where(mask, grad, 0.0).astype(BF16)
    raw = dot(masked, act_ref[...]).astype(BF16)
    raw_ref[...] = raw
    warm = warm_ref[...].reshape(n, warm_ref.shape[2])
    high = warm.astype(BF16)
    middle, low = halves(warm - high.astype(F32))
    split = jnp.concatenate([high, middle, low], axis=0)
    of_raw = dot_rows(split, raw)
    of_raw = of_raw[:n] + (of_raw[n : 2 * n] + of_raw[2 * n :])
    carried_high, carried_low = halves(padded(err_ref[0, 0], err_ref[0, 1]))
    of_err = dot_rows(split[: 2 * n], carried_high)
    of_err = of_err[:n] + (of_err[n:] + dot_rows(high, carried_low))
    left = lane < HALF
    row = lax.broadcasted_iota(jnp.int32, (rank, 128), 0)
    at_count = jnp.logical_and(row == 0, lane == 127)
    top = jnp.where(at_count, count, jnp.where(left, of_raw[:rank], of_raw[rank:]))
    bottom = jnp.where(left, of_err[:rank], of_err[rank:])
    pay_ref[...] = jnp.broadcast_to(jnp.concatenate([top, bottom], axis=0)[None], pay_ref.shape)


def basis_of(vectors):
    row = lax.broadcasted_iota(jnp.int32, (vectors.shape[0], 1), 0)
    for r in range(vectors.shape[0]):
        current = vectors[r : r + 1]
        dots = jnp.sum(vectors * current, axis=1, keepdims=True)
        norm = jnp.sqrt(dots[r : r + 1]) + 1e-08
        unit = current / norm
        later = vectors - (dots / norm) * unit
        vectors = jnp.where(row == r, unit, jnp.where(row > r, later, vectors))
    return vectors


def factor_of(pay_ref, all_tokens):
    return all_tokens / pay_ref[0:1, 127:128]


def right_kernel(all_tokens, pay_ref, raw_ref, err_ref, left_ref, basis_ref, q_ref):
    rank = pay_ref.shape[0] // 2
    hidden = err_ref.shape[2]
    factor = factor_of(pay_ref, all_tokens)
    lane = lax.broadcasted_iota(jnp.int32, (1, 128), 1)
    p_sum = factor * pay_ref[:rank] + pay_ref[rank:]
    first = basis_of(jnp.where(lane < hidden, p_sum, 0.0))
    of_second = jnp.logical_and(lane >= HALF, lane < HALF + hidden)
    second = basis_of(jnp.where(of_second, p_sum, 0.0))
    left_ref[0] = first[:, :hidden]
    left_ref[1] = pltpu.roll(second, HALF, 1)[:, :hidden]
    basis = jnp.concatenate([first, second], axis=0)
    basis_ref[...] = basis
    high, low = halves(basis)
    top = jnp.concatenate([high, high], axis=1)
    bottom = jnp.concatenate([low, jnp.zeros_like(low)], axis=1)
    lhs = jnp.concatenate([top, bottom], axis=0)
    width = q_ref.shape[2]
    for part in range(raw_ref.shape[1] // TILE):
        at = pl.ds(part * TILE, TILE)
        carried = padded(err_ref[0, 0, :, at], err_ref[0, 1, :, at])
        high, low = halves(factor * raw_ref[:, at].astype(F32) + carried)
        both = dot(lhs, jnp.concatenate([high, low], axis=0))
        q_local = both[: 2 * rank] + both[2 * rank :]
        for block in range(TILE // width):
            q_ref[part * (TILE // width) + block] = q_local[:, block * width : (block + 1) * width]


def error_kernel(
    all_tokens, workers, pay_ref, basis_ref, sum_ref, raw_ref, err_ref, right_hbm, new_hbm,
    right_ref, new_ref, sems,
):
    rank = pay_ref.shape[0] // 2
    hidden = err_ref.shape[2]
    width = sum_ref.shape[2]
    high, low = halves(basis_ref[...])
    high, low = high.astype(F32), low.astype(F32)
    gap = jnp.zeros((128 - 6 * rank, 128), F32)
    lhs = jnp.concatenate([high, high, low, gap], axis=0).T.astype(BF16)
    factor = factor_of(pay_ref, all_tokens)
    copies = []
    for part in range(raw_ref.shape[1] // TILE):
        at = pl.ds(part * TILE, TILE)
        blocks = TILE // width
        summed = jnp.concatenate([sum_ref[part * blocks + block] for block in range(blocks)], axis=1)
        right_ref[0, :, at] = summed[:rank]
        right_ref[1, :, at] = summed[rank:]
        copies.append(pltpu.make_async_copy(right_ref.at[:, :, at], right_hbm.at[:, :, at], sems.at[0, part]))
        copies[-1].start()
        high, low = halves(summed * (1.0 / workers))
        gap = jnp.zeros((128 - 6 * rank, TILE), BF16)
        approx = dot(lhs, jnp.concatenate([high, low, high, gap], axis=0))
        for matrix in range(2):
            rows = slice(matrix * HALF, matrix * HALF + HALF)
            raw = raw_ref[rows, at].astype(F32)[:hidden]
            new_ref[0, matrix, :, at] = factor * raw + err_ref[0, matrix, :, at] - approx[rows][:hidden]
        copies.append(pltpu.make_async_copy(new_ref.at[:, :, :, at], new_hbm.at[:, :, :, at], sems.at[1, part]))
        copies[-1].start()
    for each in copies:
        each.wait()


def exchange(blocks, axis):
    return lax.all_to_all(blocks, axis, 0, 0, tiled=True)


def everyone(block, axis):
    return exchange(jnp.broadcast_to(block[None], (lax.axis_size(axis),) + block.shape), axis)


ANY = pl.BlockSpec(memory_space=pl.ANY)
VMEM = pl.BlockSpec(memory_space=pltpu.VMEM)
LIMIT = 16 * 2**20


def terms(copies, lengths, labels, grad, activations, error_state, warm_start):
    _, rank, features = warm_start.shape
    operands = (labels, grad, activations, error_state, warm_start)
    raw = jax.ShapeDtypeStruct((2 * HALF, features), BF16)
    payload = jax.ShapeDtypeStruct((copies, 2 * rank, 128), F32)

    def once(x):
        return pl.BlockSpec(x.shape, lambda i: (0,) * len(x.shape))

    return pl.pallas_call(
        terms_kernel,
        grid=(1,),
        in_specs=[pl.BlockSpec(memory_space=pltpu.SMEM)] + [once(x) for x in operands],
        out_specs=[once(raw), once(payload)],
        out_shape=[raw, payload],
        name="terms",
    )(lengths, *operands)


def right(all_tokens, outer, payload, raw, error_state):
    rank = payload.shape[0] // 2
    hidden, features = error_state.shape[2:]
    return pl.pallas_call(
        functools.partial(right_kernel, all_tokens),
        in_specs=[VMEM] * 3,
        out_specs=[VMEM] * 3,
        out_shape=[
            jax.ShapeDtypeStruct((2, rank, hidden), F32),
            jax.ShapeDtypeStruct((2 * rank, 128), F32),
            jax.ShapeDtypeStruct((outer, 2 * rank, features // outer), F32),
        ],
        compiler_params=pltpu.CompilerParams(vmem_limit_bytes=LIMIT),
        name="right",
    )(payload, raw, error_state)


def error(all_tokens, workers, payload, basis, summed, raw, error_state):
    rank = payload.shape[0] // 2
    features = error_state.shape[3]
    right_factor = jax.ShapeDtypeStruct((2, rank, features), F32)
    return pl.pallas_call(
        functools.partial(error_kernel, all_tokens, workers),
        in_specs=[VMEM] * 5,
        out_specs=[ANY] * 2,
        out_shape=[right_factor, jax.ShapeDtypeStruct(error_state.shape, F32)],
        scratch_shapes=[
            pltpu.VMEM(right_factor.shape, F32),
            pltpu.VMEM(error_state.shape, F32),
            pltpu.SemaphoreType.DMA((2, features // TILE)),
        ],
        compiler_params=pltpu.CompilerParams(vmem_limit_bytes=LIMIT),
        name="error",
    )(payload, basis, summed, raw, error_state)


def local(activations, grad_hidden, labels, lengths, error_state, warm_start):
    chips = lax.axis_size("chip")
    outer = 2 * chips
    workers = lax.axis_size("replica") * outer
    all_tokens = float(activations.shape[0] * workers)
    raw, payload = terms(
        chips, lengths, labels.reshape(1, -1), grad_hidden.T, activations, error_state, warm_start
    )
    half = jnp.sum(exchange(payload.reshape(outer, -1, 128), OUTER), axis=0)
    half = jnp.sum(everyone(half, "replica"), axis=0)
    payload = lax.all_gather(half, "core", axis=0, tiled=True)
    left_rows, basis, q_local = right(all_tokens, outer, payload, raw, error_state)
    block = jnp.sum(exchange(q_local, OUTER), axis=0)
    block = jnp.sum(everyone(block, "replica"), axis=0)
    summed = everyone(block, OUTER)
    right_factor, new_error = error(
        all_tokens, workers, payload, basis, summed, raw, error_state
    )
    return (left_rows.transpose(0, 2, 1), right_factor, new_error)


def solution(mesh):
    replicas, outer = mesh.devices.shape
    split = Mesh(mesh.devices.reshape(replicas, outer // 2, 2), ("replica", "chip", "core"))
    placed = (
        P(ALL, None),
        P(ALL, None),
        P(ALL),
        P(ALL, None),
        P(ALL, None, None, None),
        P(),
    )
    return jax.shard_map(
        local,
        mesh=split,
        in_specs=placed,
        out_specs=(P(), P(), P(ALL, None, None, None)),
        check_vma=False,
    )
```

```python
import functools

import jax
import jax.numpy as jnp
from jax import lax
from jax.experimental import pallas as pl
from jax.experimental.pallas import tpu as pltpu
from jax.sharding import Mesh, PartitionSpec as P

ALL = ("replica", "chip", "core")
OUTER = ("chip", "core")
F32, BF16 = jnp.float32, jnp.bfloat16
HALF = 64
TILE = 1024


def halves(x):
    high = x.astype(BF16)
    return high, (x - high.astype(F32)).astype(BF16)


def padded(first, second):
    gap = jnp.zeros((HALF - first.shape[0], first.shape[1]), first.dtype)
    return jnp.concatenate([first, gap, second, gap], axis=0)


def dot(a, b):
    return lax.dot_general(a, b, (((1,), (0,)), ((), ())), preferred_element_type=F32)


def dot_rows(a, b):
    return lax.dot_general(a, b, (((1,), (1,)), ((), ())), preferred_element_type=F32)


def masked_rows(lengths, labels, grad):
    documents = lengths.shape[1]
    square = (documents, documents)
    upto = lax.broadcasted_iota(jnp.int32, square, 1) <= lax.broadcasted_iota(jnp.int32, square, 0)
    ends = jnp.sum(jnp.where(upto, lengths.astype(F32), 0.0), axis=1, keepdims=True)
    place = lax.broadcasted_iota(jnp.int32, (1, labels.shape[1]), 1).astype(F32)
    at_final = jnp.max(jnp.where(place == ends - 1.0, 1.0, 0.0), axis=0, keepdims=True)
    mask = jnp.logical_and(labels != -100, at_final == 0.0)
    hidden = grad.shape[0] // 2
    grad = grad.astype(F32)
    rows = padded(grad[:hidden], grad[hidden:])
    return mask, jnp.where(mask, rows, 0.0).astype(BF16)


def terms_kernel(len_ref, label_ref, grad_ref, act_ref, err_ref, warm_ref, pay_ref):
    rank = warm_ref.shape[1]
    n = 2 * rank
    mask, masked = masked_rows(len_ref[...], label_ref[...], grad_ref[...])
    count = jnp.sum(mask.astype(F32), axis=1, keepdims=True)
    raw = dot(masked, act_ref[...]).astype(BF16)
    warm = warm_ref[...].reshape(n, warm_ref.shape[2])
    high = warm.astype(BF16)
    middle, low = halves(warm - high.astype(F32))
    split = jnp.concatenate([high, middle, low], axis=0)
    of_raw = dot_rows(split, raw)
    of_raw = of_raw[:n] + (of_raw[n : 2 * n] + of_raw[2 * n :])
    carried_high, carried_low = halves(padded(err_ref[0, 0], err_ref[0, 1]))
    of_err = dot_rows(split[: 2 * n], carried_high)
    of_err = of_err[:n] + (of_err[n:] + dot_rows(high, carried_low))
    lane = lax.broadcasted_iota(jnp.int32, (1, 128), 1)
    left = lane < HALF
    row = lax.broadcasted_iota(jnp.int32, (rank, 128), 0)
    at_count = jnp.logical_and(row == 0, lane == 127)
    top = jnp.where(at_count, count, jnp.where(left, of_raw[:rank], of_raw[rank:]))
    bottom = jnp.where(left, of_err[:rank], of_err[rank:])
    pay_ref[...] = jnp.broadcast_to(jnp.concatenate([top, bottom], axis=0)[None], pay_ref.shape)


def basis_of(vectors):
    row = lax.broadcasted_iota(jnp.int32, (vectors.shape[0], 1), 0)
    for r in range(vectors.shape[0]):
        current = vectors[r : r + 1]
        dots = jnp.sum(vectors * current, axis=1, keepdims=True)
        norm = jnp.sqrt(dots[r : r + 1]) + 1e-08
        unit = current / norm
        later = vectors - (dots / norm) * unit
        vectors = jnp.where(row == r, unit, jnp.where(row > r, later, vectors))
    return vectors


def factor_of(pay_ref, all_tokens):
    return all_tokens / pay_ref[0:1, 127:128]


def right_kernel(
    all_tokens, pay_ref, len_ref, label_ref, grad_ref, act_ref, err_ref,
    left_ref, basis_ref, q_ref, raw_ref,
):
    rank = pay_ref.shape[0] // 2
    hidden = err_ref.shape[2]
    factor = factor_of(pay_ref, all_tokens)
    _, masked = masked_rows(len_ref[...], label_ref[...], grad_ref[...])
    for part in range(raw_ref.shape[1] // TILE):
        at = pl.ds(part * TILE, TILE)
        raw_ref[:, at] = dot(masked, act_ref[:, at]).astype(BF16)
    lane = lax.broadcasted_iota(jnp.int32, (1, 128), 1)
    p_sum = factor * pay_ref[:rank] + pay_ref[rank:]
    first = basis_of(jnp.where(lane < hidden, p_sum, 0.0))
    of_second = jnp.logical_and(lane >= HALF, lane < HALF + hidden)
    second = basis_of(jnp.where(of_second, p_sum, 0.0))
    left_ref[0] = first[:, :hidden]
    left_ref[1] = pltpu.roll(second, HALF, 1)[:, :hidden]
    basis = jnp.concatenate([first, second], axis=0)
    basis_ref[...] = basis
    high, low = halves(basis)
    top = jnp.concatenate([high, high], axis=1)
    bottom = jnp.concatenate([low, jnp.zeros_like(low)], axis=1)
    lhs = jnp.concatenate([top, bottom], axis=0)
    width = q_ref.shape[2]
    for part in range(raw_ref.shape[1] // TILE):
        at = pl.ds(part * TILE, TILE)
        carried = padded(err_ref[0, 0, :, at], err_ref[0, 1, :, at])
        high, low = halves(factor * raw_ref[:, at].astype(F32) + carried)
        both = dot(lhs, jnp.concatenate([high, low], axis=0))
        q_local = both[: 2 * rank] + both[2 * rank :]
        for block in range(TILE // width):
            q_ref[part * (TILE // width) + block] = q_local[:, block * width : (block + 1) * width]


def error_kernel(
    all_tokens, workers, pay_ref, basis_ref, sum_ref, len_ref, label_ref, grad_ref, act_ref,
    err_ref, right_hbm, new_hbm, right_ref, new_ref, raw_ref, sems,
):
    rank = pay_ref.shape[0] // 2
    hidden = err_ref.shape[2]
    width = sum_ref.shape[2]
    _, masked = masked_rows(len_ref[...], label_ref[...], grad_ref[...])
    for part in range(raw_ref.shape[1] // TILE):
        at = pl.ds(part * TILE, TILE)
        raw_ref[:, at] = dot(masked, act_ref[:, at]).astype(BF16)
    high, low = halves(basis_ref[...])
    high, low = high.astype(F32), low.astype(F32)
    gap = jnp.zeros((128 - 6 * rank, 128), F32)
    lhs = jnp.concatenate([high, high, low, gap], axis=0).T.astype(BF16)
    factor = factor_of(pay_ref, all_tokens)
    copies = []
    for part in range(raw_ref.shape[1] // TILE):
        at = pl.ds(part * TILE, TILE)
        blocks = TILE // width
        summed = jnp.concatenate([sum_ref[part * blocks + block] for block in range(blocks)], axis=1)
        right_ref[0, :, at] = summed[:rank]
        right_ref[1, :, at] = summed[rank:]
        copies.append(pltpu.make_async_copy(right_ref.at[:, :, at], right_hbm.at[:, :, at], sems.at[0, part]))
        copies[-1].start()
        high, low = halves(summed * (1.0 / workers))
        gap = jnp.zeros((128 - 6 * rank, TILE), BF16)
        approx = dot(lhs, jnp.concatenate([high, low, high, gap], axis=0))
        for matrix in range(2):
            rows = slice(matrix * HALF, matrix * HALF + HALF)
            raw = raw_ref[rows, at].astype(F32)[:hidden]
            new_ref[0, matrix, :, at] = factor * raw + err_ref[0, matrix, :, at] - approx[rows][:hidden]
        copies.append(pltpu.make_async_copy(new_ref.at[:, :, :, at], new_hbm.at[:, :, :, at], sems.at[1, part]))
        copies[-1].start()
    for each in copies:
        each.wait()


def exchange(blocks, axis):
    return lax.all_to_all(blocks, axis, 0, 0, tiled=True)


def everyone(block, axis):
    return exchange(jnp.broadcast_to(block[None], (lax.axis_size(axis),) + block.shape), axis)


ANY = pl.BlockSpec(memory_space=pl.ANY)
VMEM = pl.BlockSpec(memory_space=pltpu.VMEM)
LIMIT = 16 * 2**20


def terms(copies, lengths, labels, grad, activations, error_state, warm_start):
    rank = warm_start.shape[1]
    operands = (lengths, labels, grad, activations, error_state, warm_start)
    payload = jax.ShapeDtypeStruct((copies, 2 * rank, 128), F32)

    def once(x):
        return pl.BlockSpec(x.shape, lambda i: (0,) * len(x.shape))

    return pl.pallas_call(
        terms_kernel,
        grid=(1,),
        in_specs=[once(x) for x in operands],
        out_specs=once(payload),
        out_shape=payload,
        name="terms",
    )(*operands)


def right(all_tokens, outer, payload, lengths, labels, grad, activations, error_state):
    rank = payload.shape[0] // 2
    hidden, features = error_state.shape[2:]
    return pl.pallas_call(
        functools.partial(right_kernel, all_tokens),
        in_specs=[VMEM] * 6,
        out_specs=[VMEM] * 3,
        out_shape=[
            jax.ShapeDtypeStruct((2, rank, hidden), F32),
            jax.ShapeDtypeStruct((2 * rank, 128), F32),
            jax.ShapeDtypeStruct((outer, 2 * rank, features // outer), F32),
        ],
        scratch_shapes=[pltpu.VMEM((2 * HALF, features), BF16)],
        compiler_params=pltpu.CompilerParams(vmem_limit_bytes=LIMIT),
        name="right",
    )(payload, lengths, labels, grad, activations, error_state)


def error(all_tokens, workers, payload, basis, summed, lengths, labels, grad, activations, error_state):
    rank = payload.shape[0] // 2
    features = error_state.shape[3]
    right_factor = jax.ShapeDtypeStruct((2, rank, features), F32)
    return pl.pallas_call(
        functools.partial(error_kernel, all_tokens, workers),
        in_specs=[VMEM] * 8,
        out_specs=[ANY] * 2,
        out_shape=[right_factor, jax.ShapeDtypeStruct(error_state.shape, F32)],
        scratch_shapes=[
            pltpu.VMEM(right_factor.shape, F32),
            pltpu.VMEM(error_state.shape, F32),
            pltpu.VMEM((2 * HALF, features), BF16),
            pltpu.SemaphoreType.DMA((2, features // TILE)),
        ],
        compiler_params=pltpu.CompilerParams(vmem_limit_bytes=LIMIT),
        name="error",
    )(payload, basis, summed, lengths, labels, grad, activations, error_state)


def local(activations, grad_hidden, labels, lengths, error_state, warm_start):
    chips = lax.axis_size("chip")
    outer = 2 * chips
    workers = lax.axis_size("replica") * outer
    all_tokens = float(activations.shape[0] * workers)
    tokens = (lengths, labels.reshape(1, -1), grad_hidden.T, activations)
    payload = terms(chips, *tokens, error_state, warm_start)
    half = jnp.sum(exchange(payload.reshape(outer, -1, 128), OUTER), axis=0)
    half = jnp.sum(everyone(half, "replica"), axis=0)
    payload = lax.all_gather(half, "core", axis=0, tiled=True)
    left_rows, basis, q_local = right(all_tokens, outer, payload, *tokens, error_state)
    block = jnp.sum(exchange(q_local, OUTER), axis=0)
    block = jnp.sum(everyone(block, "replica"), axis=0)
    summed = everyone(block, OUTER)
    right_factor, new_error = error(
        all_tokens, workers, payload, basis, summed, *tokens, error_state
    )
    return (left_rows.transpose(0, 2, 1), right_factor, new_error)


def solution(mesh):
    replicas, outer = mesh.devices.shape
    split = Mesh(mesh.devices.reshape(replicas, outer // 2, 2), ("replica", "chip", "core"))
    placed = (
        P(ALL, None),
        P(ALL, None),
        P(ALL),
        P(ALL, None),
        P(ALL, None, None, None),
        P(),
    )
    return jax.shard_map(
        local,
        mesh=split,
        in_specs=placed,
        out_specs=(P(), P(), P(ALL, None, None, None)),
        check_vma=False,
    )
```

```python
import functools

import jax
import jax.numpy as jnp
from jax import lax
from jax.experimental import pallas as pl
from jax.experimental.pallas import tpu as pltpu
from jax.sharding import Mesh, PartitionSpec as P

ALL = ("replica", "chip", "core")
OUTER = ("chip", "core")
F32, BF16 = jnp.float32, jnp.bfloat16
HALF = 64
TILE = 1024


def halves(x):
    high = x.astype(BF16)
    return high, (x - high.astype(F32)).astype(BF16)


def padded(first, second):
    gap = jnp.zeros((HALF - first.shape[0], first.shape[1]), first.dtype)
    return jnp.concatenate([first, gap, second, gap], axis=0)


def dot(a, b):
    return lax.dot_general(a, b, (((1,), (0,)), ((), ())), preferred_element_type=F32)


def dot_rows(a, b):
    return lax.dot_general(a, b, (((1,), (1,)), ((), ())), preferred_element_type=F32)


def masked_rows(lengths, labels, grad):
    documents = lengths.shape[1]
    square = (documents, documents)
    upto = lax.broadcasted_iota(jnp.int32, square, 1) <= lax.broadcasted_iota(jnp.int32, square, 0)
    ends = jnp.sum(jnp.where(upto, lengths.astype(F32), 0.0), axis=1, keepdims=True)
    place = lax.broadcasted_iota(jnp.int32, (1, labels.shape[1]), 1).astype(F32)
    at_final = jnp.max(jnp.where(place == ends - 1.0, 1.0, 0.0), axis=0, keepdims=True)
    mask = jnp.logical_and(labels != -100, at_final == 0.0)
    hidden = grad.shape[0] // 2
    grad = grad.astype(F32)
    rows = padded(grad[:hidden], grad[hidden:])
    return mask, jnp.where(mask, rows, 0.0).astype(BF16)


def terms_kernel(len_ref, label_ref, grad_ref, act_ref, err_ref, warm_ref, pay_ref):
    rank = warm_ref.shape[1]
    n = 2 * rank
    mask, masked = masked_rows(len_ref[...], label_ref[...], grad_ref[...])
    count = jnp.sum(mask.astype(F32), axis=1, keepdims=True)
    raw = dot(masked, act_ref[...]).astype(BF16)
    warm = warm_ref[...].reshape(n, warm_ref.shape[2])
    high = warm.astype(BF16)
    middle, low = halves(warm - high.astype(F32))
    split = jnp.concatenate([high, middle, low], axis=0)
    of_raw = dot_rows(split, raw)
    of_raw = of_raw[:n] + (of_raw[n : 2 * n] + of_raw[2 * n :])
    carried_high, carried_low = halves(padded(err_ref[0, 0], err_ref[0, 1]))
    of_err = dot_rows(split[: 2 * n], carried_high)
    of_err = of_err[:n] + (of_err[n:] + dot_rows(high, carried_low))
    lane = lax.broadcasted_iota(jnp.int32, (1, 128), 1)
    left = lane < HALF
    row = lax.broadcasted_iota(jnp.int32, (rank, 128), 0)
    at_count = jnp.logical_and(row == 0, lane == 127)
    top = jnp.where(at_count, count, jnp.where(left, of_raw[:rank], of_raw[rank:]))
    bottom = jnp.where(left, of_err[:rank], of_err[rank:])
    pay_ref[...] = jnp.broadcast_to(jnp.concatenate([top, bottom], axis=0)[None], pay_ref.shape)


def basis_of(vectors):
    row = lax.broadcasted_iota(jnp.int32, (vectors.shape[0], 1), 0)
    for r in range(vectors.shape[0]):
        current = vectors[r : r + 1]
        dots = jnp.sum(vectors * current, axis=1, keepdims=True)
        norm = jnp.sqrt(dots[r : r + 1]) + 1e-08
        unit = current / norm
        later = vectors - (dots / norm) * unit
        vectors = jnp.where(row == r, unit, jnp.where(row > r, later, vectors))
    return vectors


def factor_of(pay_ref, all_tokens):
    return all_tokens / pay_ref[0:1, 127:128]


def right_kernel(
    all_tokens, pay_ref, len_ref, label_ref, grad_ref, act_ref, err_ref,
    basis_ref, q_ref, raw_ref,
):
    rank = pay_ref.shape[0] // 2
    hidden = err_ref.shape[2]
    factor = factor_of(pay_ref, all_tokens)
    _, masked = masked_rows(len_ref[...], label_ref[...], grad_ref[...])
    for part in range(raw_ref.shape[1] // TILE):
        at = pl.ds(part * TILE, TILE)
        raw_ref[:, at] = dot(masked, act_ref[:, at]).astype(BF16)
    lane = lax.broadcasted_iota(jnp.int32, (1, 128), 1)
    p_sum = factor * pay_ref[:rank] + pay_ref[rank:]
    first = basis_of(jnp.where(lane < hidden, p_sum, 0.0))
    of_second = jnp.logical_and(lane >= HALF, lane < HALF + hidden)
    second = basis_of(jnp.where(of_second, p_sum, 0.0))
    basis = jnp.concatenate([first, second], axis=0)
    basis_ref[...] = basis
    high, low = halves(basis)
    top = jnp.concatenate([high, high], axis=1)
    bottom = jnp.concatenate([low, jnp.zeros_like(low)], axis=1)
    lhs = jnp.concatenate([top, bottom], axis=0)
    width = q_ref.shape[2]
    for part in range(raw_ref.shape[1] // TILE):
        at = pl.ds(part * TILE, TILE)
        carried = padded(err_ref[0, 0, :, at], err_ref[0, 1, :, at])
        high, low = halves(factor * raw_ref[:, at].astype(F32) + carried)
        both = dot(lhs, jnp.concatenate([high, low], axis=0))
        q_local = both[: 2 * rank] + both[2 * rank :]
        for block in range(TILE // width):
            q_ref[part * (TILE // width) + block] = q_local[:, block * width : (block + 1) * width]


def error_kernel(
    all_tokens, workers, pay_ref, basis_ref, sum_ref, len_ref, label_ref, grad_ref, act_ref,
    err_ref, left_hbm, right_hbm, new_hbm, left_ref, right_ref, new_ref, sems,
):
    rank = pay_ref.shape[0] // 2
    hidden = err_ref.shape[2]
    width = sum_ref.shape[2]
    _, masked = masked_rows(len_ref[...], label_ref[...], grad_ref[...])
    basis = basis_ref[...]
    left_ref[0] = basis[:rank, :hidden]
    left_ref[1] = pltpu.roll(basis[rank:], HALF, 1)[:, :hidden]
    copies = [pltpu.make_async_copy(left_ref, left_hbm, sems.at[2, 0])]
    copies[0].start()
    high, low = halves(basis)
    high, low = high.astype(F32), low.astype(F32)
    gap = jnp.zeros((128 - 6 * rank, 128), F32)
    lhs = jnp.concatenate([high, high, low, gap], axis=0).T.astype(BF16)
    factor = factor_of(pay_ref, all_tokens)
    for part in range(act_ref.shape[1] // TILE):
        at = pl.ds(part * TILE, TILE)
        full = dot(masked, act_ref[:, at]).astype(BF16).astype(F32)
        blocks = TILE // width
        summed = jnp.concatenate([sum_ref[part * blocks + block] for block in range(blocks)], axis=1)
        right_ref[0, :, at] = summed[:rank]
        right_ref[1, :, at] = summed[rank:]
        copies.append(pltpu.make_async_copy(right_ref.at[:, :, at], right_hbm.at[:, :, at], sems.at[0, part]))
        copies[-1].start()
        high, low = halves(summed * (1.0 / workers))
        gap = jnp.zeros((128 - 6 * rank, TILE), BF16)
        approx = dot(lhs, jnp.concatenate([high, low, high, gap], axis=0))
        for matrix in range(2):
            rows = slice(matrix * HALF, matrix * HALF + HALF)
            raw = full[rows][:hidden]
            new_ref[0, matrix, :, at] = factor * raw + err_ref[0, matrix, :, at] - approx[rows][:hidden]
        copies.append(pltpu.make_async_copy(new_ref.at[:, :, :, at], new_hbm.at[:, :, :, at], sems.at[1, part]))
        copies[-1].start()
    for each in copies:
        each.wait()


def exchange(blocks, axis):
    return lax.all_to_all(blocks, axis, 0, 0, tiled=True)


def everyone(block, axis):
    return exchange(jnp.broadcast_to(block[None], (lax.axis_size(axis),) + block.shape), axis)


ANY = pl.BlockSpec(memory_space=pl.ANY)
VMEM = pl.BlockSpec(memory_space=pltpu.VMEM)
LIMIT = 16 * 2**20


def terms(copies, lengths, labels, grad, activations, error_state, warm_start):
    rank = warm_start.shape[1]
    operands = (lengths, labels, grad, activations, error_state, warm_start)
    payload = jax.ShapeDtypeStruct((copies, 2 * rank, 128), F32)

    def once(x):
        return pl.BlockSpec(x.shape, lambda i: (0,) * len(x.shape))

    return pl.pallas_call(
        terms_kernel,
        grid=(1,),
        in_specs=[once(x) for x in operands],
        out_specs=once(payload),
        out_shape=payload,
        name="terms",
    )(*operands)


def right(all_tokens, outer, payload, lengths, labels, grad, activations, error_state):
    rank = payload.shape[0] // 2
    features = error_state.shape[3]
    return pl.pallas_call(
        functools.partial(right_kernel, all_tokens),
        in_specs=[VMEM] * 6,
        out_specs=[VMEM] * 2,
        out_shape=[
            jax.ShapeDtypeStruct((2 * rank, 128), F32),
            jax.ShapeDtypeStruct((outer, 2 * rank, features // outer), F32),
        ],
        scratch_shapes=[pltpu.VMEM((2 * HALF, features), BF16)],
        compiler_params=pltpu.CompilerParams(vmem_limit_bytes=LIMIT),
        name="right",
    )(payload, lengths, labels, grad, activations, error_state)


def error(all_tokens, workers, payload, basis, summed, lengths, labels, grad, activations, error_state):
    rank = payload.shape[0] // 2
    hidden, features = error_state.shape[2:]
    left_factor = jax.ShapeDtypeStruct((2, rank, hidden), F32)
    right_factor = jax.ShapeDtypeStruct((2, rank, features), F32)
    return pl.pallas_call(
        functools.partial(error_kernel, all_tokens, workers),
        in_specs=[VMEM] * 8,
        out_specs=[ANY] * 3,
        out_shape=[left_factor, right_factor, jax.ShapeDtypeStruct(error_state.shape, F32)],
        scratch_shapes=[
            pltpu.VMEM(left_factor.shape, F32),
            pltpu.VMEM(right_factor.shape, F32),
            pltpu.VMEM(error_state.shape, F32),
            pltpu.SemaphoreType.DMA((3, features // TILE)),
        ],
        compiler_params=pltpu.CompilerParams(vmem_limit_bytes=LIMIT),
        name="error",
    )(payload, basis, summed, lengths, labels, grad, activations, error_state)


def local(activations, grad_hidden, labels, lengths, error_state, warm_start):
    chips = lax.axis_size("chip")
    outer = 2 * chips
    workers = lax.axis_size("replica") * outer
    all_tokens = float(activations.shape[0] * workers)
    tokens = (lengths, labels.reshape(1, -1), grad_hidden.T, activations)
    payload = terms(chips, *tokens, error_state, warm_start)
    half = jnp.sum(exchange(payload.reshape(outer, -1, 128), OUTER), axis=0)
    half = jnp.sum(everyone(half, "replica"), axis=0)
    payload = lax.all_gather(half, "core", axis=0, tiled=True)
    basis, q_local = right(all_tokens, outer, payload, *tokens, error_state)
    block = jnp.sum(exchange(q_local, OUTER), axis=0)
    block = jnp.sum(everyone(block, "replica"), axis=0)
    summed = everyone(block, OUTER)
    left_rows, right_factor, new_error = error(
        all_tokens, workers, payload, basis, summed, *tokens, error_state
    )
    return (left_rows.transpose(0, 2, 1), right_factor, new_error)


def solution(mesh):
    replicas, outer = mesh.devices.shape
    split = Mesh(mesh.devices.reshape(replicas, outer // 2, 2), ("replica", "chip", "core"))
    placed = (
        P(ALL, None),
        P(ALL, None),
        P(ALL),
        P(ALL, None),
        P(ALL, None, None, None),
        P(),
    )
    return jax.shard_map(
        local,
        mesh=split,
        in_specs=placed,
        out_specs=(P(), P(), P(ALL, None, None, None)),
        check_vma=False,
    )
```

```python
import functools

import jax
import jax.numpy as jnp
from jax import lax
from jax.experimental import pallas as pl
from jax.experimental.pallas import tpu as pltpu
from jax.sharding import Mesh, PartitionSpec as P

ALL = ("far", "near", "chip", "core")
REPLICA = ("far", "near")
OUTER = ("chip", "core")
PAIR = ("near", "chip", "core")
F32, BF16 = jnp.float32, jnp.bfloat16
HALF = 64
TILE = 1024


def halves(x):
    high = x.astype(BF16)
    return high, (x - high.astype(F32)).astype(BF16)


def padded(first, second):
    gap = jnp.zeros((HALF - first.shape[0], first.shape[1]), first.dtype)
    return jnp.concatenate([first, gap, second, gap], axis=0)


def dot(a, b):
    return lax.dot_general(a, b, (((1,), (0,)), ((), ())), preferred_element_type=F32)


def dot_rows(a, b):
    return lax.dot_general(a, b, (((1,), (1,)), ((), ())), preferred_element_type=F32)


def masked_rows(lengths, labels, grad):
    documents = lengths.shape[1]
    square = (documents, documents)
    upto = lax.broadcasted_iota(jnp.int32, square, 1) <= lax.broadcasted_iota(jnp.int32, square, 0)
    ends = jnp.sum(jnp.where(upto, lengths.astype(F32), 0.0), axis=1, keepdims=True)
    place = lax.broadcasted_iota(jnp.int32, (1, labels.shape[1]), 1).astype(F32)
    at_final = jnp.max(jnp.where(place == ends - 1.0, 1.0, 0.0), axis=0, keepdims=True)
    mask = jnp.logical_and(labels != -100, at_final == 0.0)
    hidden = grad.shape[0] // 2
    grad = grad.astype(F32)
    rows = padded(grad[:hidden], grad[hidden:])
    return mask, jnp.where(mask, rows, 0.0).astype(BF16)


def terms_kernel(len_ref, label_ref, grad_ref, act_ref, err_ref, warm_ref, pay_ref):
    rank = warm_ref.shape[1]
    n = 2 * rank
    mask, masked = masked_rows(len_ref[...], label_ref[...], grad_ref[...])
    count = jnp.sum(mask.astype(F32), axis=1, keepdims=True)
    raw = dot(masked, act_ref[...]).astype(BF16)
    warm = warm_ref[...].reshape(n, warm_ref.shape[2])
    high = warm.astype(BF16)
    middle, low = halves(warm - high.astype(F32))
    split = jnp.concatenate([high, middle, low], axis=0)
    of_raw = dot_rows(split, raw)
    of_raw = of_raw[:n] + (of_raw[n : 2 * n] + of_raw[2 * n :])
    carried_high, carried_low = halves(padded(err_ref[0, 0], err_ref[0, 1]))
    of_err = dot_rows(split[: 2 * n], carried_high)
    of_err = of_err[:n] + (of_err[n:] + dot_rows(high, carried_low))
    lane = lax.broadcasted_iota(jnp.int32, (1, 128), 1)
    left = lane < HALF
    row = lax.broadcasted_iota(jnp.int32, (rank, 128), 0)
    at_count = jnp.logical_and(row == 0, lane == 127)
    top = jnp.where(at_count, count, jnp.where(left, of_raw[:rank], of_raw[rank:]))
    bottom = jnp.where(left, of_err[:rank], of_err[rank:])
    pay_ref[...] = jnp.broadcast_to(jnp.concatenate([top, bottom], axis=0)[None], pay_ref.shape)


def basis_of(vectors):
    row = lax.broadcasted_iota(jnp.int32, (vectors.shape[0], 1), 0)
    for r in range(vectors.shape[0]):
        current = vectors[r : r + 1]
        dots = jnp.sum(vectors * current, axis=1, keepdims=True)
        norm = jnp.sqrt(dots[r : r + 1]) + 1e-08
        unit = current / norm
        later = vectors - (dots / norm) * unit
        vectors = jnp.where(row == r, unit, jnp.where(row > r, later, vectors))
    return vectors


def factor_of(pay_ref, all_tokens):
    return all_tokens / pay_ref[0:1, 127:128]


def right_kernel(
    all_tokens, pay_ref, len_ref, label_ref, grad_ref, act_ref, err_ref,
    basis_ref, q_ref, raw_ref,
):
    rank = pay_ref.shape[0] // 2
    hidden = err_ref.shape[2]
    factor = factor_of(pay_ref, all_tokens)
    _, masked = masked_rows(len_ref[...], label_ref[...], grad_ref[...])
    for part in range(raw_ref.shape[1] // TILE):
        at = pl.ds(part * TILE, TILE)
        raw_ref[:, at] = dot(masked, act_ref[:, at]).astype(BF16)
    lane = lax.broadcasted_iota(jnp.int32, (1, 128), 1)
    p_sum = factor * pay_ref[:rank] + pay_ref[rank:]
    first = basis_of(jnp.where(lane < hidden, p_sum, 0.0))
    of_second = jnp.logical_and(lane >= HALF, lane < HALF + hidden)
    second = basis_of(jnp.where(of_second, p_sum, 0.0))
    basis = jnp.concatenate([first, second], axis=0)
    basis_ref[...] = basis
    high, low = halves(basis)
    top = jnp.concatenate([high, high], axis=1)
    bottom = jnp.concatenate([low, jnp.zeros_like(low)], axis=1)
    lhs = jnp.concatenate([top, bottom], axis=0)
    width = q_ref.shape[3]
    for part in range(raw_ref.shape[1] // TILE):
        at = pl.ds(part * TILE, TILE)
        carried = padded(err_ref[0, 0, :, at], err_ref[0, 1, :, at])
        high, low = halves(factor * raw_ref[:, at].astype(F32) + carried)
        both = dot(lhs, jnp.concatenate([high, low], axis=0))
        q_local = both[: 2 * rank] + both[2 * rank :]
        for block in range(TILE // width):
            columns = q_local[:, block * width : (block + 1) * width]
            q_ref[0, part * (TILE // width) + block] = columns[:rank]
            q_ref[1, part * (TILE // width) + block] = columns[rank:]


def error_kernel(
    all_tokens, workers, pay_ref, basis_ref, sum_ref, len_ref, label_ref, grad_ref, act_ref,
    err_ref, left_hbm, right_hbm, new_hbm, left_ref, right_ref, new_ref, sems,
):
    rank = pay_ref.shape[0] // 2
    hidden = err_ref.shape[2]
    width = sum_ref.shape[3]
    _, masked = masked_rows(len_ref[...], label_ref[...], grad_ref[...])
    basis = basis_ref[...]
    left_ref[0] = basis[:rank, :hidden]
    left_ref[1] = pltpu.roll(basis[rank:], HALF, 1)[:, :hidden]
    copies = [pltpu.make_async_copy(left_ref, left_hbm, sems.at[2, 0])]
    copies[0].start()
    high, low = halves(basis)
    high, low = high.astype(F32), low.astype(F32)
    gap = jnp.zeros((128 - 6 * rank, 128), F32)
    lhs = jnp.concatenate([high, high, low, gap], axis=0).T.astype(BF16)
    factor = factor_of(pay_ref, all_tokens)
    for part in range(act_ref.shape[1] // TILE):
        at = pl.ds(part * TILE, TILE)
        full = dot(masked, act_ref[:, at]).astype(BF16).astype(F32)
        blocks = TILE // width
        summed = [
            jnp.concatenate([sum_ref[matrix, part * blocks + block] for block in range(blocks)], axis=1)
            for matrix in range(2)
        ]
        summed = jnp.concatenate(summed, axis=0)
        right_ref[0, :, at] = summed[:rank]
        right_ref[1, :, at] = summed[rank:]
        copies.append(pltpu.make_async_copy(right_ref.at[:, :, at], right_hbm.at[:, :, at], sems.at[0, part]))
        copies[-1].start()
        high, low = halves(summed * (1.0 / workers))
        gap = jnp.zeros((128 - 6 * rank, TILE), BF16)
        approx = dot(lhs, jnp.concatenate([high, low, high, gap], axis=0))
        for matrix in range(2):
            rows = slice(matrix * HALF, matrix * HALF + HALF)
            raw = full[rows][:hidden]
            new_ref[0, matrix, :, at] = factor * raw + err_ref[0, matrix, :, at] - approx[rows][:hidden]
        copies.append(pltpu.make_async_copy(new_ref.at[:, :, :, at], new_hbm.at[:, :, :, at], sems.at[1, part]))
        copies[-1].start()
    for each in copies:
        each.wait()


def exchange(blocks, axis):
    return lax.all_to_all(blocks, axis, 0, 0, tiled=True)


def everyone(block, axis):
    return exchange(jnp.broadcast_to(block[None], (lax.axis_size(axis),) + block.shape), axis)


ANY = pl.BlockSpec(memory_space=pl.ANY)
VMEM = pl.BlockSpec(memory_space=pltpu.VMEM)
LIMIT = 16 * 2**20


def terms(copies, lengths, labels, grad, activations, error_state, warm_start):
    rank = warm_start.shape[1]
    operands = (lengths, labels, grad, activations, error_state, warm_start)
    payload = jax.ShapeDtypeStruct((copies, 2 * rank, 128), F32)

    def once(x):
        return pl.BlockSpec(x.shape, lambda i: (0,) * len(x.shape))

    return pl.pallas_call(
        terms_kernel,
        grid=(1,),
        in_specs=[once(x) for x in operands],
        out_specs=once(payload),
        out_shape=payload,
        name="terms",
    )(*operands)


def right(all_tokens, outer, payload, lengths, labels, grad, activations, error_state):
    rank = payload.shape[0] // 2
    features = error_state.shape[3]
    return pl.pallas_call(
        functools.partial(right_kernel, all_tokens),
        in_specs=[VMEM] * 6,
        out_specs=[VMEM] * 2,
        out_shape=[
            jax.ShapeDtypeStruct((2 * rank, 128), F32),
            jax.ShapeDtypeStruct((2, outer, rank, features // outer), F32),
        ],
        scratch_shapes=[pltpu.VMEM((2 * HALF, features), BF16)],
        compiler_params=pltpu.CompilerParams(vmem_limit_bytes=LIMIT),
        name="right",
    )(payload, lengths, labels, grad, activations, error_state)


def error(all_tokens, workers, payload, basis, summed, lengths, labels, grad, activations, error_state):
    rank = payload.shape[0] // 2
    hidden, features = error_state.shape[2:]
    left_factor = jax.ShapeDtypeStruct((2, rank, hidden), F32)
    right_factor = jax.ShapeDtypeStruct((2, rank, features), F32)
    return pl.pallas_call(
        functools.partial(error_kernel, all_tokens, workers),
        in_specs=[VMEM] * 8,
        out_specs=[ANY] * 3,
        out_shape=[left_factor, right_factor, jax.ShapeDtypeStruct(error_state.shape, F32)],
        scratch_shapes=[
            pltpu.VMEM(left_factor.shape, F32),
            pltpu.VMEM(right_factor.shape, F32),
            pltpu.VMEM(error_state.shape, F32),
            pltpu.SemaphoreType.DMA((3, features // TILE)),
        ],
        compiler_params=pltpu.CompilerParams(vmem_limit_bytes=LIMIT),
        name="error",
    )(payload, basis, summed, lengths, labels, grad, activations, error_state)


def local(activations, grad_hidden, labels, lengths, error_state, warm_start):
    chips = lax.axis_size("chip")
    outer = 2 * chips
    workers = lax.axis_size(ALL)
    all_tokens = float(activations.shape[0] * workers)
    tokens = (lengths, labels.reshape(1, -1), grad_hidden.T, activations)
    payload = terms(chips, *tokens, error_state, warm_start)
    half = jnp.sum(exchange(payload.reshape(outer, -1, 128), OUTER), axis=0)
    half = jnp.sum(everyone(half, REPLICA), axis=0)
    payload = lax.all_gather(half, "core", axis=0, tiled=True)
    basis, q_local = right(all_tokens, outer, payload, *tokens, error_state)
    _, _, rank, width = q_local.shape
    block = jnp.sum(exchange(q_local.reshape(-1, rank, width), PAIR), axis=0)
    block = jnp.sum(everyone(block, "far"), axis=0)
    summed = everyone(block, PAIR).reshape(q_local.shape)
    left_rows, right_factor, new_error = error(
        all_tokens, workers, payload, basis, summed, *tokens, error_state
    )
    return (left_rows.transpose(0, 2, 1), right_factor, new_error)


def solution(mesh):
    replicas, outer = mesh.devices.shape
    split = Mesh(mesh.devices.reshape(replicas // 2, 2, outer // 2, 2), ALL)
    placed = (
        P(ALL, None),
        P(ALL, None),
        P(ALL),
        P(ALL, None),
        P(ALL, None, None, None),
        P(),
    )
    return jax.shard_map(
        local,
        mesh=split,
        in_specs=placed,
        out_specs=(P(), P(), P(ALL, None, None, None)),
        check_vma=False,
    )
```

```python
import functools

import jax
import jax.numpy as jnp
from jax import lax
from jax.experimental import pallas as pl
from jax.experimental.pallas import tpu as pltpu
from jax.sharding import Mesh, PartitionSpec as P

ALL = ("replica", "chip", "core")
OUTER = ("chip", "core")
F32, BF16 = jnp.float32, jnp.bfloat16
HALF = 64
TILE = 1024


def halves(x):
    high = x.astype(BF16)
    return high, (x - high.astype(F32)).astype(BF16)


def padded(first, second):
    gap = jnp.zeros((HALF - first.shape[0], first.shape[1]), first.dtype)
    return jnp.concatenate([first, gap, second, gap], axis=0)


def dot(a, b):
    return lax.dot_general(a, b, (((1,), (0,)), ((), ())), preferred_element_type=F32)


def dot_rows(a, b):
    return lax.dot_general(a, b, (((1,), (1,)), ((), ())), preferred_element_type=F32)


def masked_rows(lengths, labels, grad):
    documents = lengths.shape[1]
    square = (documents, documents)
    upto = lax.broadcasted_iota(jnp.int32, square, 1) <= lax.broadcasted_iota(jnp.int32, square, 0)
    ends = jnp.sum(jnp.where(upto, lengths.astype(F32), 0.0), axis=1, keepdims=True)
    place = lax.broadcasted_iota(jnp.int32, (1, labels.shape[1]), 1).astype(F32)
    at_final = jnp.max(jnp.where(place == ends - 1.0, 1.0, 0.0), axis=0, keepdims=True)
    mask = jnp.logical_and(labels != -100, at_final == 0.0)
    hidden = grad.shape[0] // 2
    grad = grad.astype(F32)
    rows = padded(grad[:hidden], grad[hidden:])
    return mask, jnp.where(mask, rows, 0.0).astype(BF16)


def terms_kernel(len_ref, label_ref, grad_ref, act_ref, err_ref, warm_ref, pay_ref):
    rank = warm_ref.shape[1]
    n = 2 * rank
    mask, masked = masked_rows(len_ref[...], label_ref[...], grad_ref[...])
    count = jnp.sum(mask.astype(F32), axis=1, keepdims=True)
    raw = dot(masked, act_ref[...]).astype(BF16)
    warm = warm_ref[...].reshape(n, warm_ref.shape[2])
    high = warm.astype(BF16)
    split = jnp.concatenate([high, (warm - high.astype(F32)).astype(BF16)], axis=0)
    of_raw = dot_rows(split, raw)
    of_raw = of_raw[:n] + of_raw[n:]
    carried_high, carried_low = halves(padded(err_ref[0, 0], err_ref[0, 1]))
    of_err = dot_rows(split, carried_high)
    of_err = of_err[:n] + (of_err[n:] + dot_rows(high, carried_low))
    lane = lax.broadcasted_iota(jnp.int32, (1, 128), 1)
    left = lane < HALF
    row = lax.broadcasted_iota(jnp.int32, (rank, 128), 0)
    at_count = jnp.logical_and(row == 0, lane == 127)
    top = jnp.where(at_count, count, jnp.where(left, of_raw[:rank], of_raw[rank:]))
    bottom = jnp.where(left, of_err[:rank], of_err[rank:])
    pay_ref[...] = jnp.broadcast_to(jnp.concatenate([top, bottom], axis=0)[None], pay_ref.shape)


def basis_of(vectors):
    row = lax.broadcasted_iota(jnp.int32, (vectors.shape[0], 1), 0)
    for r in range(vectors.shape[0]):
        current = vectors[r : r + 1]
        dots = jnp.sum(vectors * current, axis=1, keepdims=True)
        norm = jnp.sqrt(dots[r : r + 1]) + 1e-08
        unit = current / norm
        later = vectors - (dots / norm) * unit
        vectors = jnp.where(row == r, unit, jnp.where(row > r, later, vectors))
    return vectors


def factor_of(pay_ref, all_tokens):
    return all_tokens / pay_ref[0:1, 127:128]


def right_kernel(
    all_tokens, pay_ref, len_ref, label_ref, grad_ref, act_ref, err_ref,
    basis_ref, q_ref, merged_ref,
):
    rank = pay_ref.shape[0] // 2
    hidden = err_ref.shape[2]
    factor = factor_of(pay_ref, all_tokens)
    _, masked = masked_rows(len_ref[...], label_ref[...], grad_ref[...])
    parts = act_ref.shape[1] // TILE
    for part in range(parts):
        at = pl.ds(part * TILE, TILE)
        raw = dot(masked, act_ref[:, at]).astype(BF16).astype(F32)
        carried = padded(err_ref[0, 0, :, at], err_ref[0, 1, :, at])
        high, low = halves(factor * raw + carried)
        merged_ref[: 2 * HALF, at] = high
        merged_ref[2 * HALF :, at] = low
    lane = lax.broadcasted_iota(jnp.int32, (1, 128), 1)
    p_sum = factor * pay_ref[:rank] + pay_ref[rank:]
    first = basis_of(jnp.where(lane < hidden, p_sum, 0.0))
    of_second = jnp.logical_and(lane >= HALF, lane < HALF + hidden)
    second = basis_of(jnp.where(of_second, p_sum, 0.0))
    basis = jnp.concatenate([first, second], axis=0)
    basis_ref[...] = basis
    high, low = halves(basis)
    top = jnp.concatenate([high, high], axis=1)
    bottom = jnp.concatenate([low, jnp.zeros_like(low)], axis=1)
    lhs = jnp.concatenate([top, bottom], axis=0)
    width = q_ref.shape[2]
    for part in range(parts):
        both = dot(lhs, merged_ref[:, part * TILE : (part + 1) * TILE])
        q_local = both[: 2 * rank] + both[2 * rank :]
        for block in range(TILE // width):
            q_ref[part * (TILE // width) + block] = q_local[:, block * width : (block + 1) * width]


def error_kernel(
    all_tokens, workers, pay_ref, basis_ref, sum_ref, len_ref, label_ref, grad_ref, act_ref,
    err_ref, left_hbm, right_hbm, new_hbm, left_ref, right_ref, new_ref, sems,
):
    rank = pay_ref.shape[0] // 2
    hidden = err_ref.shape[2]
    width = sum_ref.shape[2]
    _, masked = masked_rows(len_ref[...], label_ref[...], grad_ref[...])
    basis = basis_ref[...]
    left_ref[0] = basis[:rank, :hidden]
    left_ref[1] = pltpu.roll(basis[rank:], HALF, 1)[:, :hidden]
    copies = [pltpu.make_async_copy(left_ref, left_hbm, sems.at[2, 0])]
    copies[0].start()
    high, low = halves(basis)
    high, low = high.astype(F32), low.astype(F32)
    gap = jnp.zeros((128 - 6 * rank, 128), F32)
    lhs = jnp.concatenate([high, high, low, gap], axis=0).T.astype(BF16)
    factor = factor_of(pay_ref, all_tokens)
    for part in range(act_ref.shape[1] // TILE):
        at = pl.ds(part * TILE, TILE)
        full = dot(masked, act_ref[:, at]).astype(BF16).astype(F32)
        blocks = TILE // width
        summed = jnp.concatenate([sum_ref[part * blocks + block] for block in range(blocks)], axis=1)
        right_ref[0, :, at] = summed[:rank]
        right_ref[1, :, at] = summed[rank:]
        copies.append(pltpu.make_async_copy(right_ref.at[:, :, at], right_hbm.at[:, :, at], sems.at[0, part]))
        copies[-1].start()
        high, low = halves(summed * (1.0 / workers))
        gap = jnp.zeros((128 - 6 * rank, TILE), BF16)
        approx = dot(lhs, jnp.concatenate([high, low, high, gap], axis=0))
        for matrix in range(2):
            rows = slice(matrix * HALF, matrix * HALF + HALF)
            raw = full[rows][:hidden]
            new_ref[0, matrix, :, at] = factor * raw + err_ref[0, matrix, :, at] - approx[rows][:hidden]
        copies.append(pltpu.make_async_copy(new_ref.at[:, :, :, at], new_hbm.at[:, :, :, at], sems.at[1, part]))
        copies[-1].start()
    for each in copies:
        each.wait()


def exchange(blocks, axis):
    return lax.all_to_all(blocks, axis, 0, 0, tiled=True)


def everyone(block, axis):
    return exchange(jnp.broadcast_to(block[None], (lax.axis_size(axis),) + block.shape), axis)


ANY = pl.BlockSpec(memory_space=pl.ANY)
VMEM = pl.BlockSpec(memory_space=pltpu.VMEM)
LIMIT = 16 * 2**20


def terms(copies, lengths, labels, grad, activations, error_state, warm_start):
    rank = warm_start.shape[1]
    operands = (lengths, labels, grad, activations, error_state, warm_start)
    payload = jax.ShapeDtypeStruct((copies, 2 * rank, 128), F32)

    def once(x):
        return pl.BlockSpec(x.shape, lambda i: (0,) * len(x.shape))

    return pl.pallas_call(
        terms_kernel,
        grid=(1,),
        in_specs=[once(x) for x in operands],
        out_specs=once(payload),
        out_shape=payload,
        name="terms",
    )(*operands)


def right(all_tokens, outer, payload, lengths, labels, grad, activations, error_state):
    rank = payload.shape[0] // 2
    features = error_state.shape[3]
    return pl.pallas_call(
        functools.partial(right_kernel, all_tokens),
        in_specs=[VMEM] * 6,
        out_specs=[VMEM] * 2,
        out_shape=[
            jax.ShapeDtypeStruct((2 * rank, 128), F32),
            jax.ShapeDtypeStruct((outer, 2 * rank, features // outer), F32),
        ],
        scratch_shapes=[pltpu.VMEM((4 * HALF, features), BF16)],
        compiler_params=pltpu.CompilerParams(vmem_limit_bytes=LIMIT),
        name="right",
    )(payload, lengths, labels, grad, activations, error_state)


def error(all_tokens, workers, payload, basis, summed, lengths, labels, grad, activations, error_state):
    rank = payload.shape[0] // 2
    hidden, features = error_state.shape[2:]
    left_factor = jax.ShapeDtypeStruct((2, rank, hidden), F32)
    right_factor = jax.ShapeDtypeStruct((2, rank, features), F32)
    return pl.pallas_call(
        functools.partial(error_kernel, all_tokens, workers),
        in_specs=[VMEM] * 8,
        out_specs=[ANY] * 3,
        out_shape=[left_factor, right_factor, jax.ShapeDtypeStruct(error_state.shape, F32)],
        scratch_shapes=[
            pltpu.VMEM(left_factor.shape, F32),
            pltpu.VMEM(right_factor.shape, F32),
            pltpu.VMEM(error_state.shape, F32),
            pltpu.SemaphoreType.DMA((3, features // TILE)),
        ],
        compiler_params=pltpu.CompilerParams(vmem_limit_bytes=LIMIT),
        name="error",
    )(payload, basis, summed, lengths, labels, grad, activations, error_state)


def local(activations, grad_hidden, labels, lengths, error_state, warm_start):
    chips = lax.axis_size("chip")
    outer = 2 * chips
    workers = lax.axis_size("replica") * outer
    all_tokens = float(activations.shape[0] * workers)
    tokens = (lengths, labels.reshape(1, -1), grad_hidden.T, activations)
    payload = terms(chips, *tokens, error_state, warm_start)
    half = jnp.sum(exchange(payload.reshape(outer, -1, 128), OUTER), axis=0)
    half = jnp.sum(everyone(half, "replica"), axis=0)
    payload = lax.all_gather(half, "core", axis=0, tiled=True)
    basis, q_local = right(all_tokens, outer, payload, *tokens, error_state)
    block = jnp.sum(exchange(q_local, OUTER), axis=0)
    block = jnp.sum(everyone(block, "replica"), axis=0)
    summed = everyone(block, OUTER)
    left_rows, right_factor, new_error = error(
        all_tokens, workers, payload, basis, summed, *tokens, error_state
    )
    return (left_rows.transpose(0, 2, 1), right_factor, new_error)


def solution(mesh):
    replicas, outer = mesh.devices.shape
    split = Mesh(mesh.devices.reshape(replicas, outer // 2, 2), ("replica", "chip", "core"))
    placed = (
        P(ALL, None),
        P(ALL, None),
        P(ALL),
        P(ALL, None),
        P(ALL, None, None, None),
        P(),
    )
    return jax.shard_map(
        local,
        mesh=split,
        in_specs=placed,
        out_specs=(P(), P(), P(ALL, None, None, None)),
        check_vma=False,
    )
```

```python
import functools

import jax
import jax.numpy as jnp
from jax import lax
from jax.experimental import pallas as pl
from jax.experimental.pallas import tpu as pltpu
from jax.sharding import Mesh, PartitionSpec as P

ALL = ("replica", "chip", "core")
OUTER = ("chip", "core")
F32, BF16 = jnp.float32, jnp.bfloat16
HALF = 64
TILE = 1024


def halves(x):
    high = x.astype(BF16)
    return high, (x - high.astype(F32)).astype(BF16)


def padded(first, second):
    gap = jnp.zeros((HALF - first.shape[0], first.shape[1]), first.dtype)
    return jnp.concatenate([first, gap, second, gap], axis=0)


def dot(a, b):
    return lax.dot_general(a, b, (((1,), (0,)), ((), ())), preferred_element_type=F32)


def dot_rows(a, b):
    return lax.dot_general(a, b, (((1,), (1,)), ((), ())), preferred_element_type=F32)


def masked_rows(lengths, labels, grad):
    documents = lengths.shape[1]
    square = (documents, documents)
    upto = lax.broadcasted_iota(jnp.int32, square, 1) <= lax.broadcasted_iota(jnp.int32, square, 0)
    ends = jnp.sum(jnp.where(upto, lengths.astype(F32), 0.0), axis=1, keepdims=True)
    place = lax.broadcasted_iota(jnp.int32, (1, labels.shape[1]), 1).astype(F32)
    at_final = jnp.max(jnp.where(place == ends - 1.0, 1.0, 0.0), axis=0, keepdims=True)
    mask = jnp.logical_and(labels != -100, at_final == 0.0)
    hidden = grad.shape[0] // 2
    grad = grad.astype(F32)
    rows = padded(grad[:hidden], grad[hidden:])
    return mask, jnp.where(mask, rows, 0.0).astype(BF16)


def terms_kernel(len_ref, label_ref, grad_ref, act_ref, err_ref, warm_ref, pay_ref):
    rank = warm_ref.shape[1]
    n = 2 * rank
    mask, masked = masked_rows(len_ref[...], label_ref[...], grad_ref[...])
    count = jnp.sum(mask.astype(F32), axis=1, keepdims=True)
    raw = dot(masked, act_ref[...]).astype(BF16)
    warm = warm_ref[...].reshape(n, warm_ref.shape[2])
    high = warm.astype(BF16)
    split = jnp.concatenate([high, (warm - high.astype(F32)).astype(BF16)], axis=0)
    of_raw = dot_rows(split, raw)
    of_raw = of_raw[:n] + of_raw[n:]
    carried_high, carried_low = halves(padded(err_ref[0, 0], err_ref[0, 1]))
    of_err = dot_rows(split, carried_high)
    of_err = of_err[:n] + (of_err[n:] + dot_rows(high, carried_low))
    lane = lax.broadcasted_iota(jnp.int32, (1, 128), 1)
    left = lane < HALF
    row = lax.broadcasted_iota(jnp.int32, (rank, 128), 0)
    at_count = jnp.logical_and(row == 0, lane == 127)
    top = jnp.where(at_count, count, jnp.where(left, of_raw[:rank], of_raw[rank:]))
    bottom = jnp.where(left, of_err[:rank], of_err[rank:])
    pay_ref[...] = jnp.broadcast_to(jnp.concatenate([top, bottom], axis=0)[None], pay_ref.shape)


def basis_of(vectors):
    rank = vectors.shape[0]
    row = lax.broadcasted_iota(jnp.int32, (rank, 1), 0)
    basis = jnp.zeros_like(vectors)
    for r in range(rank):
        current = jnp.broadcast_to(vectors[r : r + 1], vectors.shape)
        own = jnp.sum(current * current, axis=1, keepdims=True)
        dots = jnp.sum(vectors * current, axis=1, keepdims=True)
        norm = jnp.sqrt(own) + 1e-08
        unit = current / norm
        basis = jnp.where(row == r, unit, basis)
        vectors = vectors - (dots / norm) * unit
    return basis


def factor_of(pay_ref, all_tokens):
    return all_tokens / pay_ref[0:1, 127:128]


def right_kernel(
    all_tokens, pay_ref, len_ref, label_ref, grad_ref, act_ref, err_ref,
    basis_ref, q_ref, merged_ref,
):
    rank = pay_ref.shape[0] // 2
    hidden = err_ref.shape[2]
    factor = factor_of(pay_ref, all_tokens)
    _, masked = masked_rows(len_ref[...], label_ref[...], grad_ref[...])
    parts = act_ref.shape[1] // TILE
    for part in range(parts):
        at = pl.ds(part * TILE, TILE)
        raw = dot(masked, act_ref[:, at]).astype(BF16).astype(F32)
        carried = padded(err_ref[0, 0, :, at], err_ref[0, 1, :, at])
        high, low = halves(factor * raw + carried)
        merged_ref[: 2 * HALF, at] = high
        merged_ref[2 * HALF :, at] = low
    lane = lax.broadcasted_iota(jnp.int32, (1, 128), 1)
    p_sum = factor * pay_ref[:rank] + pay_ref[rank:]
    first = basis_of(jnp.where(lane < hidden, p_sum, 0.0))
    of_second = jnp.logical_and(lane >= HALF, lane < HALF + hidden)
    second = basis_of(jnp.where(of_second, p_sum, 0.0))
    basis = jnp.concatenate([first, second], axis=0)
    basis_ref[...] = basis
    high, low = halves(basis)
    top = jnp.concatenate([high, high], axis=1)
    bottom = jnp.concatenate([low, jnp.zeros_like(low)], axis=1)
    lhs = jnp.concatenate([top, bottom], axis=0)
    width = q_ref.shape[2]
    for part in range(parts):
        both = dot(lhs, merged_ref[:, part * TILE : (part + 1) * TILE])
        q_local = both[: 2 * rank] + both[2 * rank :]
        for block in range(TILE // width):
            q_ref[part * (TILE // width) + block] = q_local[:, block * width : (block + 1) * width]


def error_kernel(
    all_tokens, workers, pay_ref, basis_ref, sum_ref, len_ref, label_ref, grad_ref, act_ref,
    err_ref, left_hbm, right_hbm, new_hbm, left_ref, right_ref, new_ref, sems,
):
    rank = pay_ref.shape[0] // 2
    hidden = err_ref.shape[2]
    width = sum_ref.shape[2]
    _, masked = masked_rows(len_ref[...], label_ref[...], grad_ref[...])
    basis = basis_ref[...]
    left_ref[0] = basis[:rank, :hidden]
    left_ref[1] = pltpu.roll(basis[rank:], HALF, 1)[:, :hidden]
    copies = [pltpu.make_async_copy(left_ref, left_hbm, sems.at[2, 0])]
    copies[0].start()
    high, low = halves(basis)
    high, low = high.astype(F32), low.astype(F32)
    gap = jnp.zeros((128 - 6 * rank, 128), F32)
    lhs = jnp.concatenate([high, high, low, gap], axis=0).T.astype(BF16)
    factor = factor_of(pay_ref, all_tokens)
    for part in range(act_ref.shape[1] // TILE):
        at = pl.ds(part * TILE, TILE)
        full = dot(masked, act_ref[:, at]).astype(BF16).astype(F32)
        blocks = TILE // width
        summed = jnp.concatenate([sum_ref[part * blocks + block] for block in range(blocks)], axis=1)
        right_ref[0, :, at] = summed[:rank]
        right_ref[1, :, at] = summed[rank:]
        copies.append(pltpu.make_async_copy(right_ref.at[:, :, at], right_hbm.at[:, :, at], sems.at[0, part]))
        copies[-1].start()
        high, low = halves(summed * (1.0 / workers))
        gap = jnp.zeros((128 - 6 * rank, TILE), BF16)
        approx = dot(lhs, jnp.concatenate([high, low, high, gap], axis=0))
        for matrix in range(2):
            rows = slice(matrix * HALF, matrix * HALF + HALF)
            raw = full[rows][:hidden]
            new_ref[0, matrix, :, at] = factor * raw + err_ref[0, matrix, :, at] - approx[rows][:hidden]
        copies.append(pltpu.make_async_copy(new_ref.at[:, :, :, at], new_hbm.at[:, :, :, at], sems.at[1, part]))
        copies[-1].start()
    for each in copies:
        each.wait()


def exchange(blocks, axis):
    return lax.all_to_all(blocks, axis, 0, 0, tiled=True)


def everyone(block, axis):
    return exchange(jnp.broadcast_to(block[None], (lax.axis_size(axis),) + block.shape), axis)


ANY = pl.BlockSpec(memory_space=pl.ANY)
VMEM = pl.BlockSpec(memory_space=pltpu.VMEM)
LIMIT = 16 * 2**20


def terms(copies, lengths, labels, grad, activations, error_state, warm_start):
    rank = warm_start.shape[1]
    operands = (lengths, labels, grad, activations, error_state, warm_start)
    payload = jax.ShapeDtypeStruct((copies, 2 * rank, 128), F32)

    def once(x):
        return pl.BlockSpec(x.shape, lambda i: (0,) * len(x.shape))

    return pl.pallas_call(
        terms_kernel,
        grid=(1,),
        in_specs=[once(x) for x in operands],
        out_specs=once(payload),
        out_shape=payload,
        name="terms",
    )(*operands)


def right(all_tokens, outer, payload, lengths, labels, grad, activations, error_state):
    rank = payload.shape[0] // 2
    features = error_state.shape[3]
    return pl.pallas_call(
        functools.partial(right_kernel, all_tokens),
        in_specs=[VMEM] * 6,
        out_specs=[VMEM] * 2,
        out_shape=[
            jax.ShapeDtypeStruct((2 * rank, 128), F32),
            jax.ShapeDtypeStruct((outer, 2 * rank, features // outer), F32),
        ],
        scratch_shapes=[pltpu.VMEM((4 * HALF, features), BF16)],
        compiler_params=pltpu.CompilerParams(vmem_limit_bytes=LIMIT),
        name="right",
    )(payload, lengths, labels, grad, activations, error_state)


def error(all_tokens, workers, payload, basis, summed, lengths, labels, grad, activations, error_state):
    rank = payload.shape[0] // 2
    hidden, features = error_state.shape[2:]
    left_factor = jax.ShapeDtypeStruct((2, rank, hidden), F32)
    right_factor = jax.ShapeDtypeStruct((2, rank, features), F32)
    return pl.pallas_call(
        functools.partial(error_kernel, all_tokens, workers),
        in_specs=[VMEM] * 8,
        out_specs=[ANY] * 3,
        out_shape=[left_factor, right_factor, jax.ShapeDtypeStruct(error_state.shape, F32)],
        scratch_shapes=[
            pltpu.VMEM(left_factor.shape, F32),
            pltpu.VMEM(right_factor.shape, F32),
            pltpu.VMEM(error_state.shape, F32),
            pltpu.SemaphoreType.DMA((3, features // TILE)),
        ],
        compiler_params=pltpu.CompilerParams(vmem_limit_bytes=LIMIT),
        name="error",
    )(payload, basis, summed, lengths, labels, grad, activations, error_state)


def local(activations, grad_hidden, labels, lengths, error_state, warm_start):
    chips = lax.axis_size("chip")
    outer = 2 * chips
    workers = lax.axis_size("replica") * outer
    all_tokens = float(activations.shape[0] * workers)
    tokens = (lengths, labels.reshape(1, -1), grad_hidden.T, activations)
    payload = terms(chips, *tokens, error_state, warm_start)
    half = jnp.sum(exchange(payload.reshape(outer, -1, 128), OUTER), axis=0)
    half = jnp.sum(everyone(half, "replica"), axis=0)
    payload = lax.all_gather(half, "core", axis=0, tiled=True)
    basis, q_local = right(all_tokens, outer, payload, *tokens, error_state)
    block = jnp.sum(exchange(q_local, OUTER), axis=0)
    block = jnp.sum(everyone(block, "replica"), axis=0)
    summed = everyone(block, OUTER)
    left_rows, right_factor, new_error = error(
        all_tokens, workers, payload, basis, summed, *tokens, error_state
    )
    return (left_rows.transpose(0, 2, 1), right_factor, new_error)


def solution(mesh):
    replicas, outer = mesh.devices.shape
    split = Mesh(mesh.devices.reshape(replicas, outer // 2, 2), ("replica", "chip", "core"))
    placed = (
        P(ALL, None),
        P(ALL, None),
        P(ALL),
        P(ALL, None),
        P(ALL, None, None, None),
        P(),
    )
    return jax.shard_map(
        local,
        mesh=split,
        in_specs=placed,
        out_specs=(P(), P(), P(ALL, None, None, None)),
        check_vma=False,
    )
```
